32 devices in a mesh: face: 4 (over y, x), elem: 8 (over z, core).
Axes of the slice: x: 2, y: 2, z: 4, core: 2. Of those that a mesh axis runs over, the one named last changes fastest.
Arguments:
- field_state: float32 [432, 16384], P(None, ('face', 'elem')), may hold values from -6 to 6
- day_cost: int32 [16384], P(('face', 'elem')), may hold values from 0 to 3
- heat_rate: float32 [432], replicated, may hold values from -2 to 2
- coupling: float32 [3, 16384], P(None, ('face', 'elem')), may hold values from 0.2 to 0.7
- metric: float32 [16384], P(('face', 'elem')), may hold values from 0.5 to 2
- stencil: float32 [16, 16], replicated, may hold values from -1.5 to 1.5
- phys_owner: int32 [8192, 1], P(('face', 'elem')), may hold values from 0 to 7; in each aligned block of 256 rows (0 to 255, 256 to 511, ...) at most 64 rows name the same one
- edge_table: int32 [1024, 4], P(('face', 'elem')), may hold values from 0 to 63
- kept_inverse: float32 [1296, 8192], P(None, ('face', 'elem')), may hold values from -0.6 to 1.3
- slot_inverse: float32 [1296, 16384], P(None, ('face', 'elem')), may hold values from -0.6 to 1.3
Outputs:
- new_state: float32 [432, 16384], P(None, ('face', 'elem'))
The draws below stay inside these ranges and needn't reach their ends.
Inputs may be any that keep to these rules, and one draw needn't show every extreme that they name: `phys_owner`: in each aligned block of 256 entries (the sent columns of one device) no value appears more than 64 times, and some value appears exactly 64 times.
All inputs are finite; a program needn't handle non-finite values.
Results may differ from the reference program's by a relative error of at most 0.0003.
Values sent between devices are 32-bit elements; how exact they have to be, the bound alone decides.
A program may use at most 64 MiB of HBM per device.

```python
import math
import jax
import jax.numpy as jnp
import numpy as np
from jax import lax

FIELDS = 6
LEV = 72
BLK = 18
NB = 4
NP = 4
SWEEPS = 3
RIM_E = 16
ELEM_DEV = 32
COLS_DEV = 512
SEND = 256
CAP = 64
COLUMNS = 16384
ELEMS = 1024
HALF = 8192
N_FACE = 4
N_ELEM = 8


def diagonal_rows(rows):
    row_ids = jnp.arange(rows)
    return (row_ids % (BLK * BLK) // BLK == row_ids % BLK).astype(jnp.float32)


def draw_kept_inverse(key, part):
    sub_key = jax.random.fold_in(key, 11)
    rows = NB * BLK * BLK
    spread = jax.random.normal(sub_key, (rows, COLUMNS // 2), jnp.float32) * (0.5 / math.sqrt(BLK))
    return 0.7 * diagonal_rows(rows)[:, None] + jnp.clip(spread, -0.6, 0.6)


def draw_slot_inverse(key, part):
    sub_key = jax.random.fold_in(key, 23)
    rows = NB * BLK * BLK
    spread = jax.random.normal(sub_key, (rows, COLUMNS), jnp.float32) * (0.5 / math.sqrt(BLK))
    return 0.7 * diagonal_rows(rows)[:, None] + jnp.clip(spread, -0.6, 0.6)


def touch_ends(drawn, rng, low, high):
    longest = drawn.shape.index(max(drawn.shape))
    spots = []
    for shift in (0, 1):
        where = [jax.random.randint(jax.random.fold_in(rng, axis), (), 0, length) for axis, length in enumerate(drawn.shape)]
        where[longest] = (where[longest] + shift) % drawn.shape[longest]
        spots.append(tuple(where))
    return drawn.at[spots[0]].set(low).at[spots[1]].set(high)


def steps_of(rng, shape, cuts, low, top_value):
    level = 1.0
    for position, parts in cuts:
        steps = jax.random.uniform(jax.random.fold_in(jax.random.fold_in(rng, 6), position), (parts,), jnp.float32, low / len(cuts), top_value / len(cuts))
        level = level * jnp.repeat(jnp.exp(steps), shape[position] // parts).reshape((-1,) + (1,) * (len(shape) - 1 - position))
    return level


def routed_block(own_key, own, number, rows, amount, top, bound, lean):
    order = jax.random.permutation(own_key, amount)
    packed, common = portions_of(amount, rows * top, bound, lean, True), portions_of(amount, rows * top, bound, lean, False)
    places = jnp.arange(amount)

    def named(sizes, offset_by):
        used = int((sizes > 0).sum())
        fixed = max(1, used // 4)
        moved = fixed + (places - fixed + offset_by * (used - fixed)) % max(1, amount - fixed)
        return jnp.zeros((amount,), jnp.int32).at[order[jnp.where(places < fixed, places, moved)]].set(jnp.asarray(sizes, jnp.int32))

    sizes = jnp.where(number % 4 == 0, named(packed, number // 4), named(common, number - number // 4 - 1))
    mixed = jax.random.permutation(jax.random.fold_in(own, 3), amount)
    source_of, receiver = mixed[0:amount // 2 * 2:2], mixed[1:amount // 2 * 2:2]
    room = jnp.minimum(sizes[source_of] - 1, bound - sizes[receiver]) // 2
    room = jnp.where((source_of == order[0]) | (receiver == order[0]) | (sizes[receiver] == 0), 0, jnp.maximum(room, 0))
    moved = jax.random.randint(jax.random.fold_in(own, 4), (amount // 2,), 0, 1 << 20) % (room + 1)
    sizes = sizes.at[source_of].add(-moved).at[receiver].add(moved)
    labels = jnp.searchsorted(jnp.cumsum(sizes), jnp.arange(rows * top), side="right").astype(jnp.int32)
    table = labels.reshape(top, rows).T
    table = table[jax.random.permutation(jax.random.fold_in(own, 1), rows)]
    offset_by = jax.random.randint(jax.random.fold_in(own, 2), (rows, 1), 0, top)
    return jnp.take_along_axis(table, (jnp.arange(top)[None, :] + offset_by) % top, axis=1)


def portions_of(number_of, total, bound, slope, full):
    loads = [(1 << 20) // math.isqrt(rank ** slope) + 1 for rank in range(1, number_of + 1)]
    largest = bound if full else min(bound, max(-(-total // number_of), total * loads[0] // sum(loads)))
    least = 1 if total - largest >= number_of - 1 else 0
    given, spare = [largest] + [least] * (number_of - 1), total - largest - least * (number_of - 1)
    while spare > 0:
        candidates = [i for i in range(1, number_of) if given[i] < largest] or [i for i in range(1, number_of) if given[i] < bound]
        mass, remaining = sum([loads[i] for i in candidates]), spare
        for i in candidates:
            extra = min(bound - given[i], max(1, remaining * loads[i] // mass), spare)
            given[i] = given[i] + extra
            spare = spare - extra
    return np.array(given)


def noise(stream_key, dims, scale, most, pieces=(), held_as=jnp.bfloat16):
    drawn = scale * jax.random.normal(stream_key, dims, jnp.float32)
    if pieces:
        drawn = drawn * steps_of(stream_key, dims, pieces, -0.22, 0.18)
    return jnp.clip(drawn, -most, most).astype(held_as)


def setup_inputs(seed: int = 0) -> dict:
    keys = jax.random.split(jax.random.key(seed), 11)
    field_state = noise(keys[0], (FIELDS * LEV, COLUMNS), 1.0, 6.0, ((1, 32),), jnp.float32)
    day_cost = touch_ends(jax.random.randint(keys[1], (COLUMNS,), 0, 4), jax.random.fold_in(keys[1], 1), 0, 3).astype(jnp.int32)
    heat_rate = noise(keys[2], (FIELDS * LEV,), 0.3, 2.0, (), jnp.float32)
    coupling = jnp.clip(jnp.exp(math.log(0.7) - 1.2527629 * jax.random.uniform(keys[3], (NB - 1, COLUMNS), jnp.float32) ** steps_of(keys[3], (NB - 1, COLUMNS), ((1, 32),), -0.2, 0.2)), 0.2, 0.7)
    metric = jnp.clip(jnp.exp(math.log(2.0) - 1.3862944 * jax.random.uniform(keys[4], (COLUMNS,), jnp.float32) ** steps_of(keys[4], (COLUMNS,), ((0, 32),), -0.2, 0.2)), 0.5, 2.0)
    stencil = noise(keys[5], (NP * NP, NP * NP), (NP * NP) ** -0.5, 1.5, (), jnp.float32)
    phys_owner_keys = jax.random.split(jax.random.fold_in(keys[6], 1), HALF // SEND)
    phys_owner_turns = jax.random.permutation(jax.random.fold_in(keys[6], 3), HALF // SEND)
    phys_owner = jax.vmap(lambda own, number: routed_block(jax.random.fold_in(keys[6], 2), own, number, SEND, COLS_DEV // CAP, 1, CAP, 2))(phys_owner_keys, phys_owner_turns).reshape((HALF, 1))
    edge_table = touch_ends(jax.random.randint(keys[7], (ELEMS, 4), 0, ELEM_DEV + 2 * RIM_E), jax.random.fold_in(keys[7], 1), 0, (ELEM_DEV + 2 * RIM_E) - 1).astype(jnp.int32)
    kept_inverse = draw_kept_inverse(jax.random.fold_in(keys[10], 71), 0)
    slot_inverse = draw_slot_inverse(jax.random.fold_in(keys[10], 71), 0)
    return dict(field_state=field_state, day_cost=day_cost, heat_rate=heat_rate, coupling=coupling, metric=metric, stencil=stencil, phys_owner=phys_owner, edge_table=edge_table, kept_inverse=kept_inverse, slot_inverse=slot_inverse)


VISC_COEF = 0.2


def edge_layout():
    points = np.arange(NP * NP)
    row_of = points // NP
    col_of = points % NP
    side_masks = [row_of == 0, col_of == NP - 1, row_of == NP - 1, col_of == 0]
    flip_rows = (NP - 1 - row_of) * NP + col_of
    flip_cols = row_of * NP + NP - 1 - col_of
    matches = [flip_rows, flip_cols, flip_rows, flip_cols]
    counts = 1 + sum(mask_one * 1 for mask_one in side_masks)
    return side_masks, matches, counts


def block_apply(blocks, values):
    return jnp.einsum('bijn,fbjn->fbin', blocks, values, precision=lax.Precision.HIGHEST)


def physics(source, inverse, couple):
    count_n = source.shape[1]
    values = source.reshape(FIELDS, NB, BLK, count_n)
    blocks = inverse.reshape(NB, BLK, BLK, count_n)
    state_now = block_apply(blocks, values)
    for sweep_index in range(SWEEPS):
        from_below = couple[None, :, :] * state_now[:, :-1, BLK - 1, :]
        from_above = couple[None, :, :] * state_now[:, 1:, 0, :]
        driven = values.at[:, 1:, 0, :].add(from_below)
        driven = driven.at[:, :-1, BLK - 1, :].add(from_above)
        state_now = block_apply(blocks, driven)
    return state_now.reshape(FIELDS * LEV, count_n)


def reference(field_state, day_cost, heat_rate, coupling, metric, stencil, phys_owner, edge_table, kept_inverse, slot_inverse):
    source_all = field_state + day_cost[None, :].astype(jnp.float32) * heat_rate[:, None]
    capacity = COLS_DEV // N_ELEM

    def one_device(device):
        source = lax.dynamic_slice_in_dim(source_all, device * COLS_DEV, COLS_DEV, 1)
        couple = lax.dynamic_slice_in_dim(coupling, device * COLS_DEV, COLS_DEV, 1)
        owners = lax.dynamic_slice_in_dim(phys_owner[:, 0], device * SEND, SEND, 0)
        onehot = (owners[:, None] == jnp.arange(N_ELEM, dtype=jnp.int32)[None, :]).astype(jnp.int32)
        before = jnp.cumsum(onehot, axis=0) - onehot
        rank_of = jnp.sum(before * onehot, axis=1)
        face_now = device // N_ELEM
        partner = face_now + 1 - 2 * (face_now % 2)
        slot_cols = ((partner * N_ELEM + owners) * COLS_DEV + (device % N_ELEM) * capacity + rank_of).astype(jnp.int32)
        sent_inverse = jnp.take(slot_inverse, slot_cols, axis=1)
        own_inverse = lax.dynamic_slice_in_dim(kept_inverse, device * SEND, SEND, 1)
        inverse_cols = jnp.concatenate([own_inverse, sent_inverse], axis=1)
        column_state = physics(source, inverse_cols, couple)
        tendency = column_state - source
        return source + tendency

    stacked = lax.map(one_device, jnp.arange(N_FACE * N_ELEM, dtype=jnp.int32))
    updated = jnp.transpose(stacked, (1, 0, 2)).reshape(FIELDS * LEV, COLUMNS)

    side_masks, matches, counts = edge_layout()
    element_ids = jnp.arange(ELEMS, dtype=jnp.int32)
    device_of = element_ids // ELEM_DEV
    elem_pos = device_of % N_ELEM
    neighbours = []
    for edge_side in range(4):
        offset = edge_table[:, edge_side] - RIM_E
        shifted = (elem_pos + offset // ELEM_DEV) % N_ELEM
        neighbours.append(((device_of - elem_pos + shifted) * ELEM_DEV + offset % ELEM_DEV).astype(jnp.int32))

    def laplace(values):
        element_grid = values.reshape(FIELDS, LEV, ELEMS, NP * NP)
        metric_grid = metric.reshape(ELEMS, NP * NP)

        def per_field(field_vals):
            applied = jnp.einsum('pq,leq->lep', stencil, field_vals, precision=lax.Precision.HIGHEST)
            return applied * metric_grid[None, :, :]

        return lax.map(per_field, element_grid).reshape(FIELDS * LEV, COLUMNS)

    def edge_average(values):
        element_grid = values.reshape(FIELDS, LEV, ELEMS, NP * NP)

        def per_field(field_vals):
            summed = field_vals
            for edge_side in range(4):
                picked = field_vals[:, neighbours[edge_side], :][:, :, matches[edge_side]]
                summed = summed + picked * jnp.asarray(side_masks[edge_side], jnp.float32)[None, None, :]
            return summed / jnp.asarray(counts, jnp.float32)[None, None, :]

        return lax.map(per_field, element_grid).reshape(FIELDS * LEV, COLUMNS)

    first_pass = edge_average(laplace(updated))
    second = edge_average(laplace(first_pass))
    return updated - VISC_COEF * second
```

```python
import functools

import jax
import jax.numpy as jnp
import numpy as np
from jax import lax
from jax.experimental import pallas as pl
from jax.experimental.pallas import tpu as pltpu
from jax.sharding import PartitionSpec as P

FIELDS = 6
LEV = 72
BLK = 18
NB = 4
NP = 4
PTS = NP * NP
SWEEPS = 3
RIM_E = 16
VISC_COEF = 0.2
LANES = 128
ROWS = FIELDS * LEV
HALF_ROWS = ROWS // 2
PAIRS = BLK * BLK
REC = HALF_ROWS + 8
MESH = pl.DeviceIdType.MESH
HIGHEST = lax.Precision.HIGHEST
F32 = jnp.float32
BF16 = jnp.bfloat16


def iota(shape, dim):
    return lax.broadcasted_iota(jnp.int32, shape, dim)


def split(x):
    hi = x.astype(BF16)
    lo = (x - hi.astype(F32)).astype(BF16)
    return hi, lo


def exact_dot(x, picks, dims=((1,), (0,))):
    hi, lo = split(x)
    total = lax.dot_general(hi, picks, (dims, ((), ())), preferred_element_type=F32)
    return total + lax.dot_general(lo, picks, (dims, ((), ())), preferred_element_type=F32)


def kernel(
    groups,
    field_ref, day_ref, heat_ref, couple_ref, metric_ref, stencil_ref, owner_ref, edge_ref,
    kept_hbm, slot_hbm,
    out_ref,
    kept_raw, slot_raw, slot_inv, kept_src, kept_val, send_buf, recv_buf, slot_val, slot_y0,
    ret_buf, home_buf, upd, lap1, lap2, low1, high1, low2, high2, picks, route,
    load_sem, s1_sem, r1_sem, s2_sem, r2_sem, hs_sem, hr_sem,
):
    face = lax.axis_index("face")
    me = lax.axis_index("elem")
    partner = face + 1 - 2 * lax.rem(face, 2)
    right = lax.rem(me + 1, groups)
    left = lax.rem(me + groups - 1, groups)
    cap = 512 // groups
    inv_rows = NB * PAIRS

    loads = []
    for c in range(2):
        loads.append(pltpu.make_async_copy(
            kept_hbm.at[:, pl.ds(c * LANES, LANES)], kept_raw.at[pl.ds(c * inv_rows, inv_rows)],
            load_sem.at[c]))
    for a in range(groups):
        loads.append(pltpu.make_async_copy(
            slot_hbm.at[:, pl.ds((a // 2) * LANES, LANES)],
            slot_raw.at[pl.ds(a * inv_rows, inv_rows)], load_sem.at[2 + a]))
    for one in loads:
        one.start()

    barrier = pltpu.get_barrier_semaphore()
    for o in range(groups):
        pl.semaphore_signal(barrier, inc=1, device_id=(partner, jnp.int32(o)), device_id_type=MESH)
    for o in (left, right):
        pl.semaphore_signal(barrier, inc=1, device_id=(face, o), device_id_type=MESH)

    owner = owner_ref[...]
    named = iota((groups, 256), 0) == owner
    earlier = (iota((256, 256), 0) < iota((256, 256), 1)).astype(BF16)
    before = jnp.dot(named.astype(BF16), earlier, preferred_element_type=F32)
    rank = jnp.sum(jnp.where(named, before, 0.0), axis=0, keepdims=True).astype(jnp.int32)
    spot = owner * LANES + rank
    spot2 = jnp.concatenate([spot, spot + cap], axis=1)
    route[...] = (iota((groups * LANES, 512), 0) == spot2).astype(BF16)

    outer = (((0,), (0,)), ((), ()))
    day = day_ref[...].astype(F32)
    heating = lax.dot_general(heat_ref[...], day, outer, precision=HIGHEST, preferred_element_type=F32)
    source = field_ref[...] + heating
    couple = couple_ref[...]
    sent_couple = couple[:, 256:]
    tail = jnp.concatenate(
        [jnp.concatenate([sent_couple, sent_couple], axis=1), jnp.zeros((5, 512), F32)], axis=0)
    body = jnp.concatenate([source[:HALF_ROWS, 256:], source[HALF_ROWS:, 256:]], axis=1)
    record = exact_dot(jnp.concatenate([body, tail], axis=0), route[...], ((1,), (1,)))
    for o in range(groups):
        send_buf[o] = record[:, o * LANES:(o + 1) * LANES]
    for f in range(FIELDS):
        for c in range(2):
            kept_src[pl.ds((f * 2 + c) * LEV, LEV), :] = source[
                f * LEV:(f + 1) * LEV, c * LANES:(c + 1) * LANES]

    pl.semaphore_wait(barrier, groups + 2)

    def to_owner(o):
        return pltpu.make_async_remote_copy(
            src_ref=send_buf.at[o], dst_ref=recv_buf.at[me], send_sem=s1_sem.at[o],
            recv_sem=r1_sem.at[me], device_id=(partner, o), device_id_type=MESH)

    def from_home(a):
        return pltpu.make_async_remote_copy(
            src_ref=send_buf.at[a], dst_ref=recv_buf.at[a], send_sem=s1_sem.at[a],
            recv_sem=r1_sem.at[a], device_id=(partner, a), device_id_type=MESH)

    for k in range(groups):
        to_owner(lax.rem(me + k, groups)).start()

    for one in loads[:2]:
        one.wait()

    def kept_value(j, _):
        for f in range(FIELDS):
            kept_val[f * BLK + j] = kept_src[pl.ds(f * 2 * LEV + j, 8, stride=BLK), :]
        return 0

    lax.fori_loop(0, BLK, kept_value, 0)

    def kept_m(ij):
        return kept_raw[pl.ds(ij, 8, stride=PAIRS), :]

    def kept_row(i):
        sums = [None] * FIELDS
        for j in range(BLK):
            m = kept_m(i * BLK + j)
            for f in range(FIELDS):
                term = m * kept_val[f * BLK + j]
                sums[f] = term if sums[f] is None else sums[f] + term
        return sums

    first = kept_row(0)
    last = kept_row(BLK - 1)
    ends = (kept_m(0), kept_m(BLK - 1), kept_m((BLK - 1) * BLK), kept_m(PAIRS - 1))
    gap = jnp.zeros((1, LANES), F32)
    pieces_low, pieces_high = [], []
    for c in range(2):
        rows = [couple[k:k + 1, c * LANES:(c + 1) * LANES] for k in range(NB - 1)]
        pieces_low += [gap] + rows
        pieces_high += rows + [gap]
    c_low = jnp.concatenate(pieces_low, axis=0)
    c_high = jnp.concatenate(pieces_high, axis=0)

    def kept_drive(e0, e17):
        return c_low * pltpu.roll(e17, 1, 0), c_high * pltpu.roll(e0, 7, 0)

    drives = []
    for f in range(FIELDS):
        e0, e17 = first[f], last[f]
        for _ in range(SWEEPS - 1):
            lo, hi = kept_drive(e0, e17)
            e0 = first[f] + ends[0] * lo + ends[1] * hi
            e17 = last[f] + ends[2] * lo + ends[3] * hi
        drives.append(kept_drive(e0, e17))
    for f in range(FIELDS):
        slot_y0[2 * f] = drives[f][0]
        slot_y0[2 * f + 1] = drives[f][1]

    def kept_final(i, _):
        sums = kept_row(i)
        m0, m1 = kept_m(i * BLK), kept_m(i * BLK + BLK - 1)
        for f in range(FIELDS):
            y = sums[f] + m0 * slot_y0[2 * f] + m1 * slot_y0[2 * f + 1]
            kept_src[pl.ds(f * 2 * LEV + i, 8, stride=BLK), :] = y
        return 0

    lax.fori_loop(0, BLK, kept_final, 0)
    for c in range(2):
        upd[c] = jnp.concatenate(
            [kept_src[pl.ds((f * 2 + c) * LEV, LEV), :] for f in range(FIELDS)], axis=0)

    spread = (lax.rem(iota((PTS, LANES), 1), PTS) == iota((PTS, LANES), 0)).astype(F32)
    part = jnp.dot(stencil_ref[...], spread, precision=HIGHEST, preferred_element_type=F32)
    full = lax.dot_general(part, spread, outer, precision=HIGHEST, preferred_element_type=F32)
    same = iota((LANES, LANES), 0) // PTS == iota((LANES, LANES), 1) // PTS
    operator = jnp.where(same, full, 0.0)

    def laplace(x, c):
        applied = jnp.dot(x, operator, precision=HIGHEST, preferred_element_type=F32)
        return applied * metric_ref[:, c * LANES:(c + 1) * LANES]

    def to_left(lap, high, n):
        return pltpu.make_async_remote_copy(
            src_ref=lap.at[pl.ds(0, 2)], dst_ref=high, send_sem=hs_sem.at[n], recv_sem=hr_sem.at[n],
            device_id=(face, left), device_id_type=MESH)

    def to_right(lap, low, n):
        return pltpu.make_async_remote_copy(
            src_ref=lap.at[pl.ds(2, 2)], dst_ref=low, send_sem=hs_sem.at[n], recv_sem=hr_sem.at[n],
            device_id=(face, right), device_id_type=MESH)

    for c in range(2):
        lap1[c] = laplace(upd[c], c)
    left1 = to_left(lap1, high1, 0)
    left1.start()

    col = iota((1, 512), 1)
    point = lax.rem(col, PTS)
    pi, pj = point // NP, lax.rem(point, NP)
    place = (iota((32, 512), 1) // PTS == iota((32, 512), 0)).astype(F32)
    table = jnp.dot(edge_ref[...].astype(F32), place, preferred_element_type=F32).astype(jnp.int32) * PTS
    flip_i = (NP - 1 - pi) * NP + pj
    flip_j = pi * NP + NP - 1 - pj
    vert = jnp.where(pi == 0, table[0:1] + flip_i, jnp.where(pi == NP - 1, table[2:3] + flip_i, -1))
    hori = jnp.where(pj == NP - 1, table[1:2] + flip_j, jnp.where(pj == 0, table[3:4] + flip_j, -1))
    for k in range(8):
        row = iota((LANES, 512), 0) + k * LANES
        count = (row == col + 256).astype(F32) + (row == vert).astype(F32) + (row == hori).astype(F32)
        picks[pl.ds(k * LANES, LANES), :] = count.astype(BF16)
    share = 1.0 / (1.0 + jnp.where((pi == 0) | (pi == NP - 1), 1.0, 0.0)
                   + jnp.where((pj == 0) | (pj == NP - 1), 1.0, 0.0))

    for one in loads[2:]:
        one.wait()
    plain = (iota((8, LANES), 1) < cap) == (lax.rem(iota((8, LANES), 0), 2) == 0)

    def slot_pair(step, _):
        for u in range(BLK):
            r = step * BLK + u
            x = slot_raw[pl.ds(r, 8, stride=inv_rows), :]
            slot_inv[r] = jnp.where(plain, x, pltpu.roll(x, cap, 1))
        return 0

    lax.fori_loop(0, NB * BLK, slot_pair, 0)

    for a in range(groups):
        from_home(a).wait_recv()

    recv_flat = recv_buf.reshape(groups * REC, LANES)
    ret_flat = ret_buf.reshape(groups * HALF_ROWS, LANES)

    def slot_value(step, _):
        for u in range(8):
            r = step * 8 + u
            slot_val[r] = recv_flat[pl.ds(r, 8, stride=REC), :]
        return 0

    lax.fori_loop(0, REC // 8, slot_value, 0)
    half_fields = FIELDS // 2

    def slot_row(bi, b):
        sums = [None] * half_fields
        for j in range(BLK):
            m = slot_inv[bi * BLK + j]
            for f in range(half_fields):
                term = m * slot_val[f * LEV + b * BLK + j]
                sums[f] = term if sums[f] is None else sums[f] + term
        return sums

    for b in range(NB):
        def slot_first(i, _):
            sums = slot_row(b * BLK + i, b)
            for f in range(half_fields):
                slot_y0[f * LEV + b * BLK + i] = sums[f]
            return 0

        lax.fori_loop(0, BLK, slot_first, 0)

    between = [slot_val[HALF_ROWS + k] for k in range(NB - 1)]

    def slot_drive(e0, e17):
        lo = [None] + [between[b - 1] * e17[b - 1] for b in range(1, NB)]
        hi = [between[b] * e0[b + 1] for b in range(NB - 1)] + [None]
        return lo, hi

    def driven(y, b, i, lo, hi):
        if lo is not None:
            y = y + slot_inv[(b * BLK + i) * BLK] * lo
        if hi is not None:
            y = y + slot_inv[(b * BLK + i) * BLK + BLK - 1] * hi
        return y

    for f in range(half_fields):
        e0 = [slot_y0[f * LEV + b * BLK] for b in range(NB)]
        e17 = [slot_y0[f * LEV + b * BLK + BLK - 1] for b in range(NB)]
        first, last = e0, e17
        for _ in range(SWEEPS - 1):
            lo, hi = slot_drive(e0, e17)
            e0 = [driven(first[b], b, 0, lo[b], hi[b]) for b in range(NB)]
            e17 = [driven(last[b], b, BLK - 1, lo[b], hi[b]) for b in range(NB)]
        lo, hi = slot_drive(e0, e17)

        def slot_final(i, _):
            for b in range(NB):
                r = f * LEV + b * BLK + i
                ret_flat[pl.ds(r, 8, stride=HALF_ROWS), :] = driven(slot_y0[r], b, i, lo[b], hi[b])
            return 0

        lax.fori_loop(0, BLK, slot_final, 0)

    def to_home(a):
        return pltpu.make_async_remote_copy(
            src_ref=ret_buf.at[a], dst_ref=home_buf.at[me], send_sem=s2_sem.at[a],
            recv_sem=r2_sem.at[me], device_id=(partner, a), device_id_type=MESH)

    def from_owner(o):
        return pltpu.make_async_remote_copy(
            src_ref=ret_buf.at[o], dst_ref=home_buf.at[o], send_sem=s2_sem.at[o],
            recv_sem=r2_sem.at[o], device_id=(partner, o), device_id_type=MESH)

    for k in range(groups):
        to_home(lax.rem(me + k, groups)).start()
    for o in range(groups):
        from_owner(o).wait_recv()
    home = jnp.concatenate([home_buf[o] for o in range(groups)], axis=1)
    back = exact_dot(home, route[...])
    for c in range(2):
        upd[2 + c] = jnp.concatenate(
            [back[:, c * LANES:(c + 1) * LANES], back[:, (2 + c) * LANES:(3 + c) * LANES]], axis=0)
    for c in (2, 3):
        lap1[c] = laplace(upd[c], c)
    right1 = to_right(lap1, low1, 1)
    right1.start()

    def own_sum(lap):
        mine = jnp.concatenate([lap[c] for c in range(4)], axis=1)
        return exact_dot(mine, picks[pl.ds(256, 512), :])

    def rim_sum(rim, start):
        both = jnp.concatenate([rim[0], rim[1]], axis=1)
        return exact_dot(both, picks[pl.ds(start, 256), :])

    total = own_sum(lap1)
    left1.wait_recv()
    total = total + rim_sum(high1, 768)
    right1.wait_recv()
    first_pass = (total + rim_sum(low1, 0)) * share
    left2 = to_left(lap2, high2, 2)
    right2 = to_right(lap2, low2, 3)
    for c in range(2):
        lap2[c] = laplace(first_pass[:, c * LANES:(c + 1) * LANES], c)
    left2.start()
    for c in (2, 3):
        lap2[c] = laplace(first_pass[:, c * LANES:(c + 1) * LANES], c)
    right2.start()
    total = own_sum(lap2)
    left2.wait_recv()
    total = total + rim_sum(high2, 768)
    right2.wait_recv()
    second = (total + rim_sum(low2, 0)) * share
    for c in range(4):
        out_ref[:, c * LANES:(c + 1) * LANES] = (
            upd[c] - VISC_COEF * second[:, c * LANES:(c + 1) * LANES])

    for k in range(groups):
        to_owner(jnp.int32(k)).wait_send()
        to_home(jnp.int32(k)).wait_send()
    for one in (left1, right1, left2, right2):
        one.wait_send()


def fused(field_state, day_cost, heat_rate, coupling, metric, stencil, phys_owner, edge_table,
          kept_inverse, slot_inverse):
    groups = lax.axis_size("elem")
    cols = field_state.shape[1]
    inv_rows = NB * PAIRS
    vmem = pl.BlockSpec(memory_space=pltpu.VMEM)
    anywhere = pl.BlockSpec(memory_space=pl.ANY)
    dma = pltpu.SemaphoreType.DMA
    rim = pltpu.VMEM((2, ROWS, LANES), F32)
    whole = pltpu.VMEM((4, ROWS, LANES), F32)
    return pl.pallas_call(
        functools.partial(kernel, groups),
        out_shape=jax.ShapeDtypeStruct((ROWS, cols), F32),
        in_specs=[vmem] * 8 + [anywhere] * 2,
        out_specs=vmem,
        scratch_shapes=[
            pltpu.VMEM((2 * inv_rows, LANES), F32),
            pltpu.VMEM((groups * inv_rows, LANES), F32),
            pltpu.VMEM((inv_rows, 8, LANES), F32),
            pltpu.VMEM((2 * ROWS, LANES), F32),
            pltpu.VMEM((FIELDS * BLK, 8, LANES), F32),
            pltpu.VMEM((groups, REC, LANES), F32),
            pltpu.VMEM((groups, REC, LANES), F32),
            pltpu.VMEM((REC, 8, LANES), F32),
            pltpu.VMEM((HALF_ROWS, 8, LANES), F32),
            pltpu.VMEM((groups, HALF_ROWS, LANES), F32),
            pltpu.VMEM((groups, HALF_ROWS, LANES), F32),
            whole, whole, whole,
            rim, rim, rim, rim,
            pltpu.VMEM((8 * LANES, 512), BF16),
            pltpu.VMEM((groups * LANES, 512), BF16),
            dma((2 + groups,)), dma((groups,)), dma((groups,)), dma((groups,)), dma((groups,)),
            dma((4,)), dma((4,)),
        ],
        compiler_params=pltpu.CompilerParams(
            collective_id=0, has_side_effects=True, vmem_limit_bytes=48 * 2**20),
    )(
        field_state, day_cost.reshape(1, -1), heat_rate.reshape(1, -1), coupling,
        metric.reshape(1, -1), stencil, phys_owner.reshape(1, -1), edge_table.T,
        kept_inverse, slot_inverse,
    )


def swapped(value):
    pairs = [(source, source ^ 1) for source in range(lax.axis_size("face"))]
    return lax.ppermute(value, "face", pairs)


def block_apply(blocks, values):
    result = jnp.zeros(values.shape, F32)
    for j in range(BLK):
        result = result + blocks[None, :, :, j, :] * values[:, :, j, None, :]
    return result


def physics(source, inverse, couple):
    count_n = source.shape[1]
    values = source.reshape(FIELDS, NB, BLK, count_n)
    blocks = inverse.reshape(NB, BLK, BLK, count_n)
    state = block_apply(blocks, values)
    for _ in range(SWEEPS):
        driven = values.at[:, 1:, 0, :].add(couple[None] * state[:, :-1, BLK - 1, :])
        driven = driven.at[:, :-1, BLK - 1, :].add(couple[None] * state[:, 1:, 0, :])
        state = block_apply(blocks, driven)
    return state.reshape(FIELDS * LEV, count_n)


def general(field_state, day_cost, heat_rate, coupling, metric, stencil, phys_owner, edge_table,
            kept_inverse, slot_inverse):
    cols = field_state.shape[1]
    half = cols // 2
    groups = lax.axis_size("elem")
    cap = cols // groups
    source = field_state + day_cost[None, :].astype(F32) * heat_rate[:, None]
    owners = phys_owner[:, 0]
    named = (owners[:, None] == jnp.arange(groups)[None, :]).astype(F32)
    places = jnp.arange(half)
    earlier = (places[None, :] < places[:, None]).astype(F32)
    rank = jnp.sum(jnp.dot(earlier, named, precision=HIGHEST) * named, axis=1).astype(jnp.int32)
    route = ((owners * cap + rank)[:, None] == jnp.arange(cols)[None, :]).astype(F32)
    record = jnp.concatenate([source[:, half:], coupling[:, half:]], axis=0)
    record = jnp.dot(record, route, precision=HIGHEST)
    crossed = swapped(lax.all_to_all(record, "elem", split_axis=1, concat_axis=1, tiled=True))
    done = physics(crossed[:ROWS], slot_inverse, crossed[ROWS:])
    home = lax.all_to_all(swapped(done), "elem", split_axis=1, concat_axis=1, tiled=True)
    sent = jnp.dot(home, route.T, precision=HIGHEST)
    kept = physics(source[:, :half], kept_inverse, coupling[:, :half])
    updated = jnp.concatenate([kept, sent], axis=1)
    rim = RIM_E * PTS
    point = np.arange(cols) % PTS
    pi, pj = point // NP, point % NP
    flip_i, flip_j = (NP - 1 - pi) * NP + pj, pi * NP + NP - 1 - pj
    table = jnp.repeat(edge_table, PTS, axis=0) * PTS
    rows = jnp.arange(cols + 2 * rim)[:, None]
    picks = (rows == jnp.arange(cols)[None, :] + rim).astype(F32)
    sides = ((pi == 0, flip_i), (pj == NP - 1, flip_j), (pi == NP - 1, flip_i), (pj == 0, flip_j))
    divisor = np.ones((cols,), np.float32)
    for k, (mask, match) in enumerate(sides):
        divisor = divisor + mask
        picks = picks + ((rows == (table[:, k] + match)[None, :]) & mask[None, :]).astype(F32)
    operator = jnp.kron(jnp.eye(cols // PTS, dtype=F32), stencil.T)
    ring = [(i, (i + 1) % groups) for i in range(groups)]
    back = [(b, a) for a, b in ring]

    def smooth(x):
        lap = jnp.dot(x, operator, precision=HIGHEST) * metric[None, :]
        low = lax.ppermute(lap[:, cols - rim:], "elem", ring)
        high = lax.ppermute(lap[:, :rim], "elem", back)
        extended = jnp.concatenate([low, lap, high], axis=1)
        return jnp.dot(extended, picks, precision=HIGHEST) / divisor.astype(np.float32)[None, :]

    return updated - VISC_COEF * smooth(smooth(updated))


def solution(mesh):
    in_specs = (
        P(None, ("face", "elem")),
        P(("face", "elem")),
        P(),
        P(None, ("face", "elem")),
        P(("face", "elem")),
        P(),
        P(("face", "elem"), None),
        P(("face", "elem"), None),
        P(None, ("face", "elem")),
        P(None, ("face", "elem")),
    )
    out_specs = P(None, ("face", "elem"))
    local = fused if mesh.shape["elem"] == 8 else general
    return jax.shard_map(local, mesh=mesh, in_specs=in_specs, out_specs=out_specs, check_vma=False)
```

```python
import functools

import jax
import jax.numpy as jnp
import numpy as np
from jax import lax
from jax.experimental import pallas as pl
from jax.experimental.pallas import tpu as pltpu
from jax.sharding import PartitionSpec as P

FIELDS = 6
LEV = 72
BLK = 18
NB = 4
NP = 4
PTS = NP * NP
SWEEPS = 3
RIM_E = 16
VISC_COEF = 0.2
LANES = 128
ROWS = FIELDS * LEV
PAIRS = BLK * BLK
PIECES = FIELDS // 2
MESH = pl.DeviceIdType.MESH
HIGHEST = lax.Precision.HIGHEST
F32 = jnp.float32
BF16 = jnp.bfloat16


def iota(shape, dim):
    return lax.broadcasted_iota(jnp.int32, shape, dim)


def split(x):
    hi = x.astype(BF16)
    lo = (x - hi.astype(F32)).astype(BF16)
    return hi, lo


def exact_dot(x, picks, dims=((1,), (0,))):
    hi, lo = split(x)
    both = jnp.concatenate([hi, lo], axis=0)
    total = lax.dot_general(both, picks, (dims, ((), ())), preferred_element_type=F32)
    return total[:x.shape[0]] + total[x.shape[0]:]


def kernel(
    groups,
    field_ref, day_ref, heat_ref, couple_ref, metric_ref, stencil_ref, owner_ref, edge_ref,
    kept_hbm, slot_hbm,
    out_ref,
    kept_raw, slot_raw, slot_inv, kept_src, kept_val, drive,
    send0, send1, send2, recv0, recv1, recv2, slot_val, slot_y0,
    ret0, ret1, ret2, home_buf, upd, lap1, lap2, low1, high1, low2, high2, picks, route,
    load_sem, s1_sem, r1_sem, s2_sem, r2_sem, hs_sem, hr_sem,
):
    face = lax.axis_index("face")
    me = lax.axis_index("elem")
    partner = face + 1 - 2 * lax.rem(face, 2)
    right = lax.rem(me + 1, groups)
    left = lax.rem(me + groups - 1, groups)
    cap = 512 // groups
    inv_rows = NB * PAIRS
    sends, recvs, rets = (send0, send1, send2), (recv0, recv1, recv2), (ret0, ret1, ret2)

    loads = []
    for c in range(2):
        loads.append(pltpu.make_async_copy(
            kept_hbm.at[:, pl.ds(c * LANES, LANES)], kept_raw.at[pl.ds(c * inv_rows, inv_rows)],
            load_sem.at[c]))
    for a in range(groups):
        loads.append(pltpu.make_async_copy(
            slot_hbm.at[:, pl.ds((a // 2) * LANES, LANES)],
            slot_raw.at[pl.ds(a * inv_rows, inv_rows)], load_sem.at[2 + a]))
    for one in loads:
        one.start()

    barrier = pltpu.get_barrier_semaphore()
    for o in range(groups):
        pl.semaphore_signal(barrier, inc=1, device_id=(partner, jnp.int32(o)), device_id_type=MESH)
    for o in (left, right):
        pl.semaphore_signal(barrier, inc=1, device_id=(face, o), device_id_type=MESH)

    def to_owner(o, p):
        return pltpu.make_async_remote_copy(
            src_ref=sends[p].at[o], dst_ref=recvs[p].at[me], send_sem=s1_sem.at[p, o],
            recv_sem=r1_sem.at[p, me], device_id=(partner, o), device_id_type=MESH)

    def from_home(a, p):
        return pltpu.make_async_remote_copy(
            src_ref=sends[p].at[a], dst_ref=recvs[p].at[a], send_sem=s1_sem.at[p, a],
            recv_sem=r1_sem.at[p, a], device_id=(partner, a), device_id_type=MESH)

    def to_home(a, p):
        return pltpu.make_async_remote_copy(
            src_ref=rets[p].at[a], dst_ref=home_buf.at[p, me], send_sem=s2_sem.at[p, a],
            recv_sem=r2_sem.at[p, me], device_id=(partner, a), device_id_type=MESH)

    def from_owner(o, p):
        return pltpu.make_async_remote_copy(
            src_ref=rets[p].at[o], dst_ref=home_buf.at[p, o], send_sem=s2_sem.at[p, o],
            recv_sem=r2_sem.at[p, o], device_id=(partner, o), device_id_type=MESH)

    owner = owner_ref[...]
    named = iota((groups, 256), 0) == owner
    earlier = (iota((256, 256), 0) < iota((256, 256), 1)).astype(BF16)
    before = jnp.dot(named.astype(BF16), earlier, preferred_element_type=F32)
    rank = jnp.sum(jnp.where(named, before, 0.0), axis=0, keepdims=True).astype(jnp.int32)
    spot = owner * LANES + rank
    spot2 = jnp.concatenate([spot, spot + cap], axis=1)
    route[...] = (iota((groups * LANES, 512), 0) == spot2).astype(BF16)

    outer = (((0,), (0,)), ((), ()))
    day = day_ref[...].astype(F32)
    heating = lax.dot_general(heat_ref[...], day, outer, precision=HIGHEST, preferred_element_type=F32)
    source = field_ref[...] + heating
    couple = couple_ref[...]
    sent_couple = couple[:, 256:]
    tail = jnp.concatenate(
        [jnp.concatenate([sent_couple, sent_couple], axis=1), jnp.zeros((5, 512), F32)], axis=0)
    for p in range(PIECES):
        body = jnp.concatenate(
            [source[p * LEV:(p + 1) * LEV, 256:], source[(p + 3) * LEV:(p + 4) * LEV, 256:]], axis=1)
        if p == 0:
            body = jnp.concatenate([body, tail], axis=0)
        record = exact_dot(body, route[...], ((1,), (1,)))
        for o in range(groups):
            sends[p][o] = record[:, o * LANES:(o + 1) * LANES]
        if p == 0:
            pl.semaphore_wait(barrier, groups + 2)
        for k in range(groups):
            to_owner(lax.rem(me + k, groups), p).start()
    for f in range(FIELDS):
        for c in range(2):
            kept_src[pl.ds((f * 2 + c) * LEV, LEV), :] = source[
                f * LEV:(f + 1) * LEV, c * LANES:(c + 1) * LANES]

    for one in loads[2:]:
        one.wait()
    plain = (iota((8, LANES), 1) < cap) == (lax.rem(iota((8, LANES), 0), 2) == 0)

    def slot_pair(step, _):
        for u in range(BLK):
            r = step * BLK + u
            x = slot_raw[pl.ds(r, 8, stride=inv_rows), :]
            slot_inv[r] = jnp.where(plain, x, pltpu.roll(x, cap, 1))
        return 0

    lax.fori_loop(0, NB * BLK, slot_pair, 0)

    slot_m = slot_inv

    def slot_piece(p):
        for a in range(groups):
            from_home(a, p).wait_recv()
        rows = LEV + 8 if p == 0 else LEV
        recv_flat = recvs[p].reshape(groups * rows, LANES)
        ret_flat = rets[p].reshape(groups * LEV, LANES)

        def slot_value(step, _):
            for u in range(8):
                slot_val[step * 8 + u] = recv_flat[pl.ds(step * 8 + u, 8, stride=rows), :]
            return 0

        lax.fori_loop(0, LEV // 8, slot_value, 0)
        if p == 0:
            for k in range(NB - 1):
                slot_val[LEV + k] = recv_flat[pl.ds(LEV + k, 8, stride=rows), :]

        for b in range(NB):
            values = [slot_val[b * BLK + j] for j in range(BLK)]

            def slot_first(i, _):
                sums = [slot_m[(b * BLK + i) * BLK + j] * values[j] for j in range(BLK)]
                while len(sums) > 1:
                    pairs = [sums[k] + sums[k + 1] for k in range(0, len(sums) - 1, 2)]
                    sums = pairs + sums[len(pairs) * 2:]
                slot_y0[b * BLK + i] = sums[0]
                return 0

            lax.fori_loop(0, BLK, slot_first, 0)

        between = [slot_val[LEV + k] for k in range(NB - 1)]

        def slot_drive(e0, e17):
            lo = [None] + [between[b - 1] * e17[b - 1] for b in range(1, NB)]
            hi = [between[b] * e0[b + 1] for b in range(NB - 1)] + [None]
            return lo, hi

        def driven(y, b, i, lo, hi):
            if lo is not None:
                y = y + slot_m[(b * BLK + i) * BLK] * lo
            if hi is not None:
                y = y + slot_m[(b * BLK + i) * BLK + BLK - 1] * hi
            return y

        e0 = first = [slot_y0[b * BLK] for b in range(NB)]
        e17 = last = [slot_y0[b * BLK + BLK - 1] for b in range(NB)]
        for _ in range(SWEEPS - 1):
            lo, hi = slot_drive(e0, e17)
            e0 = [driven(first[b], b, 0, lo[b], hi[b]) for b in range(NB)]
            e17 = [driven(last[b], b, BLK - 1, lo[b], hi[b]) for b in range(NB)]
        lo, hi = slot_drive(e0, e17)

        def slot_final(i, _):
            for b in range(NB):
                r = b * BLK + i
                ret_flat[pl.ds(r, 8, stride=LEV), :] = driven(slot_y0[r], b, i, lo[b], hi[b])
            return 0

        lax.fori_loop(0, BLK, slot_final, 0)
        for k in range(groups):
            to_home(lax.rem(me + k, groups), p).start()

    for p in range(PIECES):
        slot_piece(p)

    for one in loads[:2]:
        one.wait()

    def kept_value(j, _):
        for f in range(FIELDS):
            kept_val[f * BLK + j] = kept_src[pl.ds(f * 2 * LEV + j, 8, stride=BLK), :]
        return 0

    lax.fori_loop(0, BLK, kept_value, 0)

    def kept_m(ij):
        return kept_raw[pl.ds(ij, 8, stride=PAIRS), :]

    def kept_row(i):
        sums = [None] * FIELDS
        for j in range(BLK):
            m = kept_m(i * BLK + j)
            for f in range(FIELDS):
                term = m * kept_val[f * BLK + j]
                sums[f] = term if sums[f] is None else sums[f] + term
        return sums

    first = kept_row(0)
    last = kept_row(BLK - 1)
    ends = (kept_m(0), kept_m(BLK - 1), kept_m((BLK - 1) * BLK), kept_m(PAIRS - 1))
    gap = jnp.zeros((1, LANES), F32)
    pieces_low, pieces_high = [], []
    for c in range(2):
        rows = [couple[k:k + 1, c * LANES:(c + 1) * LANES] for k in range(NB - 1)]
        pieces_low += [gap] + rows
        pieces_high += rows + [gap]
    c_low = jnp.concatenate(pieces_low, axis=0)
    c_high = jnp.concatenate(pieces_high, axis=0)

    def kept_drive(e0, e17):
        return c_low * pltpu.roll(e17, 1, 0), c_high * pltpu.roll(e0, 7, 0)

    drives = []
    for f in range(FIELDS):
        e0, e17 = first[f], last[f]
        for _ in range(SWEEPS - 1):
            lo, hi = kept_drive(e0, e17)
            e0 = first[f] + ends[0] * lo + ends[1] * hi
            e17 = last[f] + ends[2] * lo + ends[3] * hi
        drives.append(kept_drive(e0, e17))
    for f in range(FIELDS):
        drive[2 * f] = drives[f][0]
        drive[2 * f + 1] = drives[f][1]

    def kept_final(i, _):
        sums = kept_row(i)
        m0, m1 = kept_m(i * BLK), kept_m(i * BLK + BLK - 1)
        for f in range(FIELDS):
            y = sums[f] + m0 * drive[2 * f] + m1 * drive[2 * f + 1]
            kept_src[pl.ds(f * 2 * LEV + i, 8, stride=BLK), :] = y
        return 0

    lax.fori_loop(0, BLK, kept_final, 0)
    for p in range(PIECES):
        for c in range(2):
            upd[p, c] = jnp.concatenate(
                [kept_src[pl.ds((f * 2 + c) * LEV, LEV), :] for f in (p, p + 3)], axis=0)

    spread = (lax.rem(iota((PTS, LANES), 1), PTS) == iota((PTS, LANES), 0)).astype(F32)
    part = jnp.dot(stencil_ref[...], spread, precision=HIGHEST, preferred_element_type=F32)
    full = lax.dot_general(part, spread, outer, precision=HIGHEST, preferred_element_type=F32)
    same = iota((LANES, LANES), 0) // PTS == iota((LANES, LANES), 1) // PTS
    operator = jnp.where(same, full, 0.0)

    def laplace(x, c):
        applied = jnp.dot(x, operator, precision=HIGHEST, preferred_element_type=F32)
        return applied * metric_ref[:, c * LANES:(c + 1) * LANES]

    def to_left(lap, high, n, p):
        return pltpu.make_async_remote_copy(
            src_ref=lap.at[p, pl.ds(0, 2)], dst_ref=high.at[p], send_sem=hs_sem.at[n, p],
            recv_sem=hr_sem.at[n, p], device_id=(face, left), device_id_type=MESH)

    def to_right(lap, low, n, p):
        return pltpu.make_async_remote_copy(
            src_ref=lap.at[p, pl.ds(2, 2)], dst_ref=low.at[p], send_sem=hs_sem.at[n, p],
            recv_sem=hr_sem.at[n, p], device_id=(face, right), device_id_type=MESH)

    for p in range(PIECES):
        for c in range(2):
            lap1[p, c] = laplace(upd[p, c], c)
        to_left(lap1, high1, 0, p).start()

    col = iota((1, 512), 1)
    point = lax.rem(col, PTS)
    pi, pj = point // NP, lax.rem(point, NP)
    place = (iota((32, 512), 1) // PTS == iota((32, 512), 0)).astype(F32)
    table = jnp.dot(edge_ref[...].astype(F32), place, preferred_element_type=F32).astype(jnp.int32) * PTS
    flip_i = (NP - 1 - pi) * NP + pj
    flip_j = pi * NP + NP - 1 - pj
    vert = jnp.where(pi == 0, table[0:1] + flip_i, jnp.where(pi == NP - 1, table[2:3] + flip_i, -1))
    hori = jnp.where(pj == NP - 1, table[1:2] + flip_j, jnp.where(pj == 0, table[3:4] + flip_j, -1))
    for k in range(8):
        row = iota((LANES, 512), 0) + k * LANES
        count = (row == col + 256).astype(F32) + (row == vert).astype(F32) + (row == hori).astype(F32)
        picks[pl.ds(k * LANES, LANES), :] = count.astype(BF16)
    share = 1.0 / (1.0 + jnp.where((pi == 0) | (pi == NP - 1), 1.0, 0.0)
                   + jnp.where((pj == 0) | (pj == NP - 1), 1.0, 0.0))

    def own_sum(lap, p):
        mine = jnp.concatenate([lap[p, c] for c in range(4)], axis=1)
        return exact_dot(mine, picks[pl.ds(256, 512), :])

    def rim_sum(rim, p, start):
        both = jnp.concatenate([rim[p, 0], rim[p, 1]], axis=1)
        return exact_dot(both, picks[pl.ds(start, 256), :])

    def at_home(p):
        for o in range(groups):
            from_owner(o, p).wait_recv()
        home = jnp.concatenate([home_buf[p, o] for o in range(groups)], axis=1)
        back = exact_dot(home, route[...])
        for c in range(2):
            upd[p, 2 + c] = jnp.concatenate(
                [back[:, c * LANES:(c + 1) * LANES], back[:, (2 + c) * LANES:(3 + c) * LANES]], axis=0)
        for c in (2, 3):
            lap1[p, c] = laplace(upd[p, c], c)
        to_right(lap1, low1, 1, p).start()

    def averaged(lap, high, low, n, p):
        total = own_sum(lap, p)
        to_left(lap, high, n, p).wait_recv()
        total = total + rim_sum(high, p, 768)
        to_right(lap, low, n + 1, p).wait_recv()
        return (total + rim_sum(low, p, 0)) * share

    def first_round(p):
        first_pass = averaged(lap1, high1, low1, 0, p)
        for c in range(4):
            lap2[p, c] = laplace(first_pass[:, c * LANES:(c + 1) * LANES], c)
        to_left(lap2, high2, 2, p).start()
        to_right(lap2, low2, 3, p).start()

    def second_round(p):
        second = averaged(lap2, high2, low2, 2, p)
        for c in range(4):
            lanes = slice(c * LANES, (c + 1) * LANES)
            new = upd[p, c] - VISC_COEF * second[:, lanes]
            out_ref[p * LEV:(p + 1) * LEV, lanes] = new[:LEV]
            out_ref[(p + 3) * LEV:(p + 4) * LEV, lanes] = new[LEV:]

    at_home(0)
    at_home(1)
    first_round(0)
    at_home(2)
    first_round(1)
    second_round(0)
    first_round(2)
    second_round(1)
    second_round(2)

    for p in range(PIECES):
        for k in range(groups):
            to_owner(jnp.int32(k), p).wait_send()
            to_home(jnp.int32(k), p).wait_send()
        for lap, low, high, n in ((lap1, low1, high1, 0), (lap2, low2, high2, 2)):
            to_left(lap, high, n, p).wait_send()
            to_right(lap, low, n + 1, p).wait_send()


def fused(field_state, day_cost, heat_rate, coupling, metric, stencil, phys_owner, edge_table,
          kept_inverse, slot_inverse):
    groups = lax.axis_size("elem")
    cols = field_state.shape[1]
    inv_rows = NB * PAIRS
    vmem = pl.BlockSpec(memory_space=pltpu.VMEM)
    anywhere = pl.BlockSpec(memory_space=pl.ANY)
    dma = pltpu.SemaphoreType.DMA
    rim = pltpu.VMEM((PIECES, 2, 2 * LEV, LANES), F32)
    whole = pltpu.VMEM((PIECES, 4, 2 * LEV, LANES), F32)
    part = pltpu.VMEM((groups, LEV, LANES), F32)
    part0 = pltpu.VMEM((groups, LEV + 8, LANES), F32)
    return pl.pallas_call(
        functools.partial(kernel, groups),
        out_shape=jax.ShapeDtypeStruct((ROWS, cols), F32),
        in_specs=[vmem] * 8 + [anywhere] * 2,
        out_specs=vmem,
        scratch_shapes=[
            pltpu.VMEM((2 * inv_rows, LANES), F32),
            pltpu.VMEM((groups * inv_rows, LANES), F32),
            pltpu.VMEM((inv_rows, 8, LANES), F32),
            pltpu.VMEM((2 * ROWS, LANES), F32),
            pltpu.VMEM((FIELDS * BLK, 8, LANES), F32),
            pltpu.VMEM((2 * FIELDS, 8, LANES), F32),
            part0, part, part, part0, part, part,
            pltpu.VMEM((LEV + 8, 8, LANES), F32),
            pltpu.VMEM((LEV, 8, LANES), F32),
            part, part, part,
            pltpu.VMEM((PIECES, groups, LEV, LANES), F32),
            whole, whole, whole,
            rim, rim, rim, rim,
            pltpu.VMEM((8 * LANES, 512), BF16),
            pltpu.VMEM((groups * LANES, 512), BF16),
            dma((2 + groups,)), dma((PIECES, groups)), dma((PIECES, groups)),
            dma((PIECES, groups)), dma((PIECES, groups)), dma((4, PIECES)), dma((4, PIECES)),
        ],
        compiler_params=pltpu.CompilerParams(
            collective_id=0, has_side_effects=True, vmem_limit_bytes=60 * 2**20),
    )(
        field_state, day_cost.reshape(1, -1), heat_rate.reshape(1, -1), coupling,
        metric.reshape(1, -1), stencil, phys_owner.reshape(1, -1), edge_table.T,
        kept_inverse, slot_inverse,
    )


def swapped(value):
    pairs = [(source, source ^ 1) for source in range(lax.axis_size("face"))]
    return lax.ppermute(value, "face", pairs)


def block_apply(blocks, values):
    result = jnp.zeros(values.shape, F32)
    for j in range(BLK):
        result = result + blocks[None, :, :, j, :] * values[:, :, j, None, :]
    return result


def physics(source, inverse, couple):
    count_n = source.shape[1]
    values = source.reshape(FIELDS, NB, BLK, count_n)
    blocks = inverse.reshape(NB, BLK, BLK, count_n)
    state = block_apply(blocks, values)
    for _ in range(SWEEPS):
        driven = values.at[:, 1:, 0, :].add(couple[None] * state[:, :-1, BLK - 1, :])
        driven = driven.at[:, :-1, BLK - 1, :].add(couple[None] * state[:, 1:, 0, :])
        state = block_apply(blocks, driven)
    return state.reshape(FIELDS * LEV, count_n)


def general(field_state, day_cost, heat_rate, coupling, metric, stencil, phys_owner, edge_table,
            kept_inverse, slot_inverse):
    cols = field_state.shape[1]
    half = cols // 2
    groups = lax.axis_size("elem")
    cap = cols // groups
    source = field_state + day_cost[None, :].astype(F32) * heat_rate[:, None]
    owners = phys_owner[:, 0]
    named = (owners[:, None] == jnp.arange(groups)[None, :]).astype(F32)
    places = jnp.arange(half)
    earlier = (places[None, :] < places[:, None]).astype(F32)
    rank = jnp.sum(jnp.dot(earlier, named, precision=HIGHEST) * named, axis=1).astype(jnp.int32)
    route = ((owners * cap + rank)[:, None] == jnp.arange(cols)[None, :]).astype(F32)
    record = jnp.concatenate([source[:, half:], coupling[:, half:]], axis=0)
    record = jnp.dot(record, route, precision=HIGHEST)
    crossed = swapped(lax.all_to_all(record, "elem", split_axis=1, concat_axis=1, tiled=True))
    done = physics(crossed[:ROWS], slot_inverse, crossed[ROWS:])
    home = lax.all_to_all(swapped(done), "elem", split_axis=1, concat_axis=1, tiled=True)
    sent = jnp.dot(home, route.T, precision=HIGHEST)
    kept = physics(source[:, :half], kept_inverse, coupling[:, :half])
    updated = jnp.concatenate([kept, sent], axis=1)
    rim = RIM_E * PTS
    point = np.arange(cols) % PTS
    pi, pj = point // NP, point % NP
    flip_i, flip_j = (NP - 1 - pi) * NP + pj, pi * NP + NP - 1 - pj
    table = jnp.repeat(edge_table, PTS, axis=0) * PTS
    rows = jnp.arange(cols + 2 * rim)[:, None]
    picks = (rows == jnp.arange(cols)[None, :] + rim).astype(F32)
    sides = ((pi == 0, flip_i), (pj == NP - 1, flip_j), (pi == NP - 1, flip_i), (pj == 0, flip_j))
    divisor = np.ones((cols,), np.float32)
    for k, (mask, match) in enumerate(sides):
        divisor = divisor + mask
        picks = picks + ((rows == (table[:, k] + match)[None, :]) & mask[None, :]).astype(F32)
    operator = jnp.kron(jnp.eye(cols // PTS, dtype=F32), stencil.T)
    ring = [(i, (i + 1) % groups) for i in range(groups)]
    back = [(b, a) for a, b in ring]

    def smooth(x):
        lap = jnp.dot(x, operator, precision=HIGHEST) * metric[None, :]
        low = lax.ppermute(lap[:, cols - rim:], "elem", ring)
        high = lax.ppermute(lap[:, :rim], "elem", back)
        extended = jnp.concatenate([low, lap, high], axis=1)
        return jnp.dot(extended, picks, precision=HIGHEST) / divisor.astype(np.float32)[None, :]

    return updated - VISC_COEF * smooth(smooth(updated))


def solution(mesh):
    in_specs = (
        P(None, ("face", "elem")),
        P(("face", "elem")),
        P(),
        P(None, ("face", "elem")),
        P(("face", "elem")),
        P(),
        P(("face", "elem"), None),
        P(("face", "elem"), None),
        P(None, ("face", "elem")),
        P(None, ("face", "elem")),
    )
    out_specs = P(None, ("face", "elem"))
    local = fused if mesh.shape["elem"] == 8 else general
    return jax.shard_map(local, mesh=mesh, in_specs=in_specs, out_specs=out_specs, check_vma=False)
```

```python
import functools

import jax
import jax.numpy as jnp
import numpy as np
from jax import lax
from jax.experimental import pallas as pl
from jax.experimental.pallas import tpu as pltpu
from jax.sharding import PartitionSpec as P

FIELDS = 6
LEV = 72
BLK = 18
NB = 4
NP = 4
PTS = NP * NP
SWEEPS = 3
RIM_E = 16
VISC_COEF = 0.2
LANES = 128
EDGE_PTS = 12
RIM = RIM_E * EDGE_PTS
ROWS = FIELDS * LEV
PAIRS = BLK * BLK
PIECES = FIELDS // 2
MESH = pl.DeviceIdType.MESH
HIGHEST = lax.Precision.HIGHEST
F32 = jnp.float32
BF16 = jnp.bfloat16


def iota(shape, dim):
    return lax.broadcasted_iota(jnp.int32, shape, dim)


def split(x):
    hi = x.astype(BF16)
    lo = (x - hi.astype(F32)).astype(BF16)
    return hi, lo


def packed(place):
    p = lax.rem(place, PTS)
    rank = jnp.where(p == 7, 5, jnp.where(p == 8, 6, jnp.where(p == 11, 7, jnp.where(p > 11, p - 4, p))))
    inside = (p == 5) | (p == 6) | (p == 9) | (p == 10)
    return jnp.where(inside, -4096, place // PTS * EDGE_PTS + rank)


def exact_dot(x, picks, dims=((1,), (0,))):
    hi, lo = split(x)
    both = jnp.concatenate([hi, lo], axis=0)
    total = lax.dot_general(both, picks, (dims, ((), ())), preferred_element_type=F32)
    return total[:x.shape[0]] + total[x.shape[0]:]


def kernel(
    groups,
    field_ref, day_ref, heat_ref, couple_ref, metric_ref, stencil_ref, owner_ref, edge_ref,
    kept_hbm, slot_hbm,
    out_ref,
    kept_raw, slot_raw, slot_inv, kept_src, kept_val, drive,
    send0, send1, send2, recv0, recv1, recv2, slot_val, slot_y0,
    ret0, ret1, ret2, home_buf, upd, lap1, lap2, low1, high1, low2, high2, out1, out2, picks, rims, pack, route,
    load_sem, s1_sem, r1_sem, s2_sem, r2_sem, hs_sem, hr_sem,
):
    face = lax.axis_index("face")
    me = lax.axis_index("elem")
    partner = face + 1 - 2 * lax.rem(face, 2)
    right = lax.rem(me + 1, groups)
    left = lax.rem(me + groups - 1, groups)
    cap = 512 // groups
    inv_rows = NB * PAIRS
    sends, recvs, rets = (send0, send1, send2), (recv0, recv1, recv2), (ret0, ret1, ret2)

    loads = []
    for c in range(2):
        loads.append(pltpu.make_async_copy(
            kept_hbm.at[:, pl.ds(c * LANES, LANES)], kept_raw.at[pl.ds(c * inv_rows, inv_rows)],
            load_sem.at[c]))
    for a in range(groups):
        loads.append(pltpu.make_async_copy(
            slot_hbm.at[:, pl.ds((a // 2) * LANES, LANES)],
            slot_raw.at[pl.ds(a * inv_rows, inv_rows)], load_sem.at[2 + a]))
    for one in loads:
        one.start()

    barrier = pltpu.get_barrier_semaphore()
    for o in range(groups):
        pl.semaphore_signal(barrier, inc=1, device_id=(partner, jnp.int32(o)), device_id_type=MESH)
    for o in (left, right):
        pl.semaphore_signal(barrier, inc=1, device_id=(face, o), device_id_type=MESH)

    def to_owner(o, p):
        return pltpu.make_async_remote_copy(
            src_ref=sends[p].at[o], dst_ref=recvs[p].at[me], send_sem=s1_sem.at[p, o],
            recv_sem=r1_sem.at[p, me], device_id=(partner, o), device_id_type=MESH)

    def from_home(a, p):
        return pltpu.make_async_remote_copy(
            src_ref=sends[p].at[a], dst_ref=recvs[p].at[a], send_sem=s1_sem.at[p, a],
            recv_sem=r1_sem.at[p, a], device_id=(partner, a), device_id_type=MESH)

    def to_home(a, p):
        return pltpu.make_async_remote_copy(
            src_ref=rets[p].at[a], dst_ref=home_buf.at[p, me], send_sem=s2_sem.at[p, a],
            recv_sem=r2_sem.at[p, me], device_id=(partner, a), device_id_type=MESH)

    def from_owner(o, p):
        return pltpu.make_async_remote_copy(
            src_ref=rets[p].at[o], dst_ref=home_buf.at[p, o], send_sem=s2_sem.at[p, o],
            recv_sem=r2_sem.at[p, o], device_id=(partner, o), device_id_type=MESH)

    owner = owner_ref[...]
    named = iota((groups, 256), 0) == owner
    earlier = (iota((256, 256), 0) < iota((256, 256), 1)).astype(BF16)
    before = jnp.dot(named.astype(BF16), earlier, preferred_element_type=F32)
    rank = jnp.sum(jnp.where(named, before, 0.0), axis=0, keepdims=True).astype(jnp.int32)
    spot = owner * LANES + rank
    spot2 = jnp.concatenate([spot, spot + cap], axis=1)
    route[...] = (iota((groups * LANES, 512), 0) == spot2).astype(BF16)

    outer = (((0,), (0,)), ((), ()))
    day = day_ref[...].astype(F32)
    heating = lax.dot_general(heat_ref[...], day, outer, precision=HIGHEST, preferred_element_type=F32)
    source = field_ref[...] + heating
    couple = couple_ref[...]
    sent_couple = couple[:, 256:]
    tail = jnp.concatenate(
        [jnp.concatenate([sent_couple, sent_couple], axis=1), jnp.zeros((5, 512), F32)], axis=0)
    for p in range(PIECES):
        body = jnp.concatenate(
            [source[p * LEV:(p + 1) * LEV, 256:], source[(p + 3) * LEV:(p + 4) * LEV, 256:]], axis=1)
        if p == 0:
            body = jnp.concatenate([body, tail], axis=0)
        record = exact_dot(body, route[...], ((1,), (1,)))
        for o in range(groups):
            sends[p][o] = record[:, o * LANES:(o + 1) * LANES]
        if p == 0:
            pl.semaphore_wait(barrier, groups + 2)
        for k in range(groups):
            to_owner(lax.rem(me + k, groups), p).start()
    for f in range(FIELDS):
        for c in range(2):
            kept_src[pl.ds((f * 2 + c) * LEV, LEV), :] = source[
                f * LEV:(f + 1) * LEV, c * LANES:(c + 1) * LANES]

    for one in loads[2:]:
        one.wait()
    plain = (iota((8, LANES), 1) < cap) == (lax.rem(iota((8, LANES), 0), 2) == 0)

    def slot_pair(step, _):
        for u in range(BLK):
            r = step * BLK + u
            x = slot_raw[pl.ds(r, 8, stride=inv_rows), :]
            slot_inv[r] = jnp.where(plain, x, pltpu.roll(x, cap, 1))
        return 0

    lax.fori_loop(0, NB * BLK, slot_pair, 0)

    slot_m = slot_inv

    def slot_piece(p):
        for a in range(groups):
            from_home(a, p).wait_recv()
        rows = LEV + 8 if p == 0 else LEV
        recv_flat = recvs[p].reshape(groups * rows, LANES)
        ret_flat = rets[p].reshape(groups * LEV, LANES)

        def slot_value(step, _):
            for u in range(8):
                slot_val[step * 8 + u] = recv_flat[pl.ds(step * 8 + u, 8, stride=rows), :]
            return 0

        lax.fori_loop(0, LEV // 8, slot_value, 0)
        if p == 0:
            for k in range(NB - 1):
                slot_val[LEV + k] = recv_flat[pl.ds(LEV + k, 8, stride=rows), :]

        for b in range(NB):
            values = [slot_val[b * BLK + j] for j in range(BLK)]

            def slot_first(i, _):
                sums = [slot_m[(b * BLK + i) * BLK + j] * values[j] for j in range(BLK)]
                while len(sums) > 1:
                    pairs = [sums[k] + sums[k + 1] for k in range(0, len(sums) - 1, 2)]
                    sums = pairs + sums[len(pairs) * 2:]
                slot_y0[b * BLK + i] = sums[0]
                return 0

            lax.fori_loop(0, BLK, slot_first, 0)

        between = [slot_val[LEV + k] for k in range(NB - 1)]

        def slot_drive(e0, e17):
            lo = [None] + [between[b - 1] * e17[b - 1] for b in range(1, NB)]
            hi = [between[b] * e0[b + 1] for b in range(NB - 1)] + [None]
            return lo, hi

        def driven(y, b, i, lo, hi):
            if lo is not None:
                y = y + slot_m[(b * BLK + i) * BLK] * lo
            if hi is not None:
                y = y + slot_m[(b * BLK + i) * BLK + BLK - 1] * hi
            return y

        e0 = first = [slot_y0[b * BLK] for b in range(NB)]
        e17 = last = [slot_y0[b * BLK + BLK - 1] for b in range(NB)]
        for _ in range(SWEEPS - 1):
            lo, hi = slot_drive(e0, e17)
            e0 = [driven(first[b], b, 0, lo[b], hi[b]) for b in range(NB)]
            e17 = [driven(last[b], b, BLK - 1, lo[b], hi[b]) for b in range(NB)]
        lo, hi = slot_drive(e0, e17)

        def slot_final(i, _):
            for b in range(NB):
                r = b * BLK + i
                ret_flat[pl.ds(r, 8, stride=LEV), :] = driven(slot_y0[r], b, i, lo[b], hi[b])
            return 0

        lax.fori_loop(0, BLK, slot_final, 0)
        for k in range(groups):
            to_home(lax.rem(me + k, groups), p).start()

    for p in range(PIECES):
        slot_piece(p)

    for one in loads[:2]:
        one.wait()

    def kept_value(j, _):
        for f in range(FIELDS):
            kept_val[f * BLK + j] = kept_src[pl.ds(f * 2 * LEV + j, 8, stride=BLK), :]
        return 0

    lax.fori_loop(0, BLK, kept_value, 0)

    def kept_m(ij):
        return kept_raw[pl.ds(ij, 8, stride=PAIRS), :]

    def kept_row(i):
        sums = [None] * FIELDS
        for j in range(BLK):
            m = kept_m(i * BLK + j)
            for f in range(FIELDS):
                term = m * kept_val[f * BLK + j]
                sums[f] = term if sums[f] is None else sums[f] + term
        return sums

    first = kept_row(0)
    last = kept_row(BLK - 1)
    ends = (kept_m(0), kept_m(BLK - 1), kept_m((BLK - 1) * BLK), kept_m(PAIRS - 1))
    gap = jnp.zeros((1, LANES), F32)
    pieces_low, pieces_high = [], []
    for c in range(2):
        rows = [couple[k:k + 1, c * LANES:(c + 1) * LANES] for k in range(NB - 1)]
        pieces_low += [gap] + rows
        pieces_high += rows + [gap]
    c_low = jnp.concatenate(pieces_low, axis=0)
    c_high = jnp.concatenate(pieces_high, axis=0)

    def kept_drive(e0, e17):
        return c_low * pltpu.roll(e17, 1, 0), c_high * pltpu.roll(e0, 7, 0)

    drives = []
    for f in range(FIELDS):
        e0, e17 = first[f], last[f]
        for _ in range(SWEEPS - 1):
            lo, hi = kept_drive(e0, e17)
            e0 = first[f] + ends[0] * lo + ends[1] * hi
            e17 = last[f] + ends[2] * lo + ends[3] * hi
        drives.append(kept_drive(e0, e17))
    for f in range(FIELDS):
        drive[2 * f] = drives[f][0]
        drive[2 * f + 1] = drives[f][1]

    def kept_final(i, _):
        sums = kept_row(i)
        m0, m1 = kept_m(i * BLK), kept_m(i * BLK + BLK - 1)
        for f in range(FIELDS):
            y = sums[f] + m0 * drive[2 * f] + m1 * drive[2 * f + 1]
            kept_src[pl.ds(f * 2 * LEV + i, 8, stride=BLK), :] = y
        return 0

    lax.fori_loop(0, BLK, kept_final, 0)
    for p in range(PIECES):
        for c in range(2):
            upd[p, c] = jnp.concatenate(
                [kept_src[pl.ds((f * 2 + c) * LEV, LEV), :] for f in (p, p + 3)], axis=0)

    spread = (lax.rem(iota((PTS, LANES), 1), PTS) == iota((PTS, LANES), 0)).astype(F32)
    part = jnp.dot(stencil_ref[...], spread, precision=HIGHEST, preferred_element_type=F32)
    full = lax.dot_general(part, spread, outer, precision=HIGHEST, preferred_element_type=F32)
    same = iota((LANES, LANES), 0) // PTS == iota((LANES, LANES), 1) // PTS
    operator = jnp.where(same, full, 0.0)

    def laplace(x, c):
        applied = jnp.dot(x, operator, precision=HIGHEST, preferred_element_type=F32)
        return applied * metric_ref[:, c * LANES:(c + 1) * LANES]

    def to_left(out, high, n, p):
        return pltpu.make_async_remote_copy(
            src_ref=out.at[0, p], dst_ref=high.at[p], send_sem=hs_sem.at[n, p],
            recv_sem=hr_sem.at[n, p], device_id=(face, left), device_id_type=MESH)

    def to_right(out, low, n, p):
        return pltpu.make_async_remote_copy(
            src_ref=out.at[1, p], dst_ref=low.at[p], send_sem=hs_sem.at[n, p],
            recv_sem=hr_sem.at[n, p], device_id=(face, right), device_id_type=MESH)

    place512 = iota((512, 2 * RIM), 0)
    place_now = lax.rem(place512, 256)
    shift = place512 // 256 * RIM
    pack[...] = (packed(place_now) + shift == iota((512, 2 * RIM), 1)).astype(BF16)

    def edges(lap, out, side, p):
        halves = [lap[p, 2 * side + c][h * LEV:(h + 1) * LEV] for h in range(2) for c in range(2)]
        mine = exact_dot(jnp.concatenate(halves, axis=1), pack[...])
        for k in range(3):
            out[side, p, k] = mine[:, k * LANES:(k + 1) * LANES]

    for p in range(PIECES):
        for c in range(2):
            lap1[p, c] = laplace(upd[p, c], c)
        edges(lap1, out1, 0, p)
        to_left(out1, high1, 0, p).start()

    col = iota((1, 512), 1)
    point = lax.rem(col, PTS)
    pi, pj = point // NP, lax.rem(point, NP)
    place = (iota((32, 512), 1) // PTS == iota((32, 512), 0)).astype(F32)
    table = jnp.dot(edge_ref[...].astype(F32), place, preferred_element_type=F32).astype(jnp.int32) * PTS
    flip_i = (NP - 1 - pi) * NP + pj
    flip_j = pi * NP + NP - 1 - pj
    vert = jnp.where(pi == 0, table[0:1] + flip_i, jnp.where(pi == NP - 1, table[2:3] + flip_i, -1))
    hori = jnp.where(pj == NP - 1, table[1:2] + flip_j, jnp.where(pj == 0, table[3:4] + flip_j, -1))
    for k in range(4):
        row = iota((LANES, 512), 0) + k * LANES
        count = ((row == col).astype(F32) + (row + 256 == vert).astype(F32)
                 + (row + 256 == hori).astype(F32))
        picks[pl.ds(k * LANES, LANES), :] = count.astype(BF16)
    for side, base in ((0, 0), (1, 768)):
        found = []
        for t in (vert, hori):
            near = (t >= base) & (t < base + 256)
            found.append(jnp.where(near, packed(jnp.where(near, t - base, 0)), -4096))
        for h in range(2):
            row = iota((256, 512), 0) - h * (256 - RIM)
            count = (row == found[0]).astype(F32) + (row == found[1]).astype(F32)
            rims[side, h] = count.astype(BF16)
    share = 1.0 / (1.0 + jnp.where((pi == 0) | (pi == NP - 1), 1.0, 0.0)
                   + jnp.where((pj == 0) | (pj == NP - 1), 1.0, 0.0))

    def own_sum(lap, p):
        mine = jnp.concatenate([lap[p, c] for c in range(4)], axis=1)
        return exact_dot(mine, picks[...])

    def rim_sum(rim, p, side):
        return jnp.concatenate([
            exact_dot(jnp.concatenate([rim[p, h], rim[p, h + 1]], axis=1), rims[side, h])
            for h in range(2)], axis=0)

    def at_home(p):
        for o in range(groups):
            from_owner(o, p).wait_recv()
        home = jnp.concatenate([home_buf[p, o] for o in range(groups)], axis=1)
        back = exact_dot(home, route[...])
        for c in range(2):
            upd[p, 2 + c] = jnp.concatenate(
                [back[:, c * LANES:(c + 1) * LANES], back[:, (2 + c) * LANES:(3 + c) * LANES]], axis=0)
        for c in (2, 3):
            lap1[p, c] = laplace(upd[p, c], c)
        edges(lap1, out1, 1, p)
        to_right(out1, low1, 1, p).start()

    def averaged(lap, out, high, low, n, p):
        total = own_sum(lap, p)
        to_left(out, high, n, p).wait_recv()
        total = total + rim_sum(high, p, 1)
        to_right(out, low, n + 1, p).wait_recv()
        return (total + rim_sum(low, p, 0)) * share

    def first_round(p):
        first_pass = averaged(lap1, out1, high1, low1, 0, p)
        for c in range(4):
            lap2[p, c] = laplace(first_pass[:, c * LANES:(c + 1) * LANES], c)
        edges(lap2, out2, 0, p)
        to_left(out2, high2, 2, p).start()
        edges(lap2, out2, 1, p)
        to_right(out2, low2, 3, p).start()

    def second_round(p):
        second = averaged(lap2, out2, high2, low2, 2, p)
        for c in range(4):
            lanes = slice(c * LANES, (c + 1) * LANES)
            new = upd[p, c] - VISC_COEF * second[:, lanes]
            out_ref[p * LEV:(p + 1) * LEV, lanes] = new[:LEV]
            out_ref[(p + 3) * LEV:(p + 4) * LEV, lanes] = new[LEV:]

    at_home(0)
    at_home(1)
    first_round(0)
    at_home(2)
    first_round(1)
    second_round(0)
    first_round(2)
    second_round(1)
    second_round(2)

    for p in range(PIECES):
        for k in range(groups):
            to_owner(jnp.int32(k), p).wait_send()
            to_home(jnp.int32(k), p).wait_send()
        for out, low, high, n in ((out1, low1, high1, 0), (out2, low2, high2, 2)):
            to_left(out, high, n, p).wait_send()
            to_right(out, low, n + 1, p).wait_send()


def fused(field_state, day_cost, heat_rate, coupling, metric, stencil, phys_owner, edge_table,
          kept_inverse, slot_inverse):
    groups = lax.axis_size("elem")
    cols = field_state.shape[1]
    inv_rows = NB * PAIRS
    vmem = pl.BlockSpec(memory_space=pltpu.VMEM)
    anywhere = pl.BlockSpec(memory_space=pl.ANY)
    dma = pltpu.SemaphoreType.DMA
    rim = pltpu.VMEM((PIECES, 3, LEV, LANES), F32)
    outgoing = pltpu.VMEM((2, PIECES, 3, LEV, LANES), F32)
    whole = pltpu.VMEM((PIECES, 4, 2 * LEV, LANES), F32)
    part = pltpu.VMEM((groups, LEV, LANES), F32)
    part0 = pltpu.VMEM((groups, LEV + 8, LANES), F32)
    return pl.pallas_call(
        functools.partial(kernel, groups),
        out_shape=jax.ShapeDtypeStruct((ROWS, cols), F32),
        in_specs=[vmem] * 8 + [anywhere] * 2,
        out_specs=vmem,
        scratch_shapes=[
            pltpu.VMEM((2 * inv_rows, LANES), F32),
            pltpu.VMEM((groups * inv_rows, LANES), F32),
            pltpu.VMEM((inv_rows, 8, LANES), F32),
            pltpu.VMEM((2 * ROWS, LANES), F32),
            pltpu.VMEM((FIELDS * BLK, 8, LANES), F32),
            pltpu.VMEM((2 * FIELDS, 8, LANES), F32),
            part0, part, part, part0, part, part,
            pltpu.VMEM((LEV + 8, 8, LANES), F32),
            pltpu.VMEM((LEV, 8, LANES), F32),
            part, part, part,
            pltpu.VMEM((PIECES, groups, LEV, LANES), F32),
            whole, whole, whole,
            rim, rim, rim, rim, outgoing, outgoing,
            pltpu.VMEM((512, 512), BF16),
            pltpu.VMEM((2, 2, 256, 512), BF16),
            pltpu.VMEM((512, 2 * RIM), BF16),
            pltpu.VMEM((groups * LANES, 512), BF16),
            dma((2 + groups,)), dma((PIECES, groups)), dma((PIECES, groups)),
            dma((PIECES, groups)), dma((PIECES, groups)), dma((4, PIECES)), dma((4, PIECES)),
        ],
        compiler_params=pltpu.CompilerParams(
            collective_id=0, has_side_effects=True, vmem_limit_bytes=60 * 2**20),
    )(
        field_state, day_cost.reshape(1, -1), heat_rate.reshape(1, -1), coupling,
        metric.reshape(1, -1), stencil, phys_owner.reshape(1, -1), edge_table.T,
        kept_inverse, slot_inverse,
    )


def swapped(value):
    pairs = [(source, source ^ 1) for source in range(lax.axis_size("face"))]
    return lax.ppermute(value, "face", pairs)


def block_apply(blocks, values):
    result = jnp.zeros(values.shape, F32)
    for j in range(BLK):
        result = result + blocks[None, :, :, j, :] * values[:, :, j, None, :]
    return result


def physics(source, inverse, couple):
    count_n = source.shape[1]
    values = source.reshape(FIELDS, NB, BLK, count_n)
    blocks = inverse.reshape(NB, BLK, BLK, count_n)
    state = block_apply(blocks, values)
    for _ in range(SWEEPS):
        driven = values.at[:, 1:, 0, :].add(couple[None] * state[:, :-1, BLK - 1, :])
        driven = driven.at[:, :-1, BLK - 1, :].add(couple[None] * state[:, 1:, 0, :])
        state = block_apply(blocks, driven)
    return state.reshape(FIELDS * LEV, count_n)


def general(field_state, day_cost, heat_rate, coupling, metric, stencil, phys_owner, edge_table,
            kept_inverse, slot_inverse):
    cols = field_state.shape[1]
    half = cols // 2
    groups = lax.axis_size("elem")
    cap = cols // groups
    source = field_state + day_cost[None, :].astype(F32) * heat_rate[:, None]
    owners = phys_owner[:, 0]
    named = (owners[:, None] == jnp.arange(groups)[None, :]).astype(F32)
    places = jnp.arange(half)
    earlier = (places[None, :] < places[:, None]).astype(F32)
    rank = jnp.sum(jnp.dot(earlier, named, precision=HIGHEST) * named, axis=1).astype(jnp.int32)
    route = ((owners * cap + rank)[:, None] == jnp.arange(cols)[None, :]).astype(F32)
    record = jnp.concatenate([source[:, half:], coupling[:, half:]], axis=0)
    record = jnp.dot(record, route, precision=HIGHEST)
    crossed = swapped(lax.all_to_all(record, "elem", split_axis=1, concat_axis=1, tiled=True))
    done = physics(crossed[:ROWS], slot_inverse, crossed[ROWS:])
    home = lax.all_to_all(swapped(done), "elem", split_axis=1, concat_axis=1, tiled=True)
    sent = jnp.dot(home, route.T, precision=HIGHEST)
    kept = physics(source[:, :half], kept_inverse, coupling[:, :half])
    updated = jnp.concatenate([kept, sent], axis=1)
    rim = RIM_E * PTS
    point = np.arange(cols) % PTS
    pi, pj = point // NP, point % NP
    flip_i, flip_j = (NP - 1 - pi) * NP + pj, pi * NP + NP - 1 - pj
    table = jnp.repeat(edge_table, PTS, axis=0) * PTS
    rows = jnp.arange(cols + 2 * rim)[:, None]
    picks = (rows == jnp.arange(cols)[None, :] + rim).astype(F32)
    sides = ((pi == 0, flip_i), (pj == NP - 1, flip_j), (pi == NP - 1, flip_i), (pj == 0, flip_j))
    divisor = np.ones((cols,), np.float32)
    for k, (mask, match) in enumerate(sides):
        divisor = divisor + mask
        picks = picks + ((rows == (table[:, k] + match)[None, :]) & mask[None, :]).astype(F32)
    operator = jnp.kron(jnp.eye(cols // PTS, dtype=F32), stencil.T)
    ring = [(i, (i + 1) % groups) for i in range(groups)]
    back = [(b, a) for a, b in ring]

    def smooth(x):
        lap = jnp.dot(x, operator, precision=HIGHEST) * metric[None, :]
        low = lax.ppermute(lap[:, cols - rim:], "elem", ring)
        high = lax.ppermute(lap[:, :rim], "elem", back)
        extended = jnp.concatenate([low, lap, high], axis=1)
        return jnp.dot(extended, picks, precision=HIGHEST) / divisor.astype(np.float32)[None, :]

    return updated - VISC_COEF * smooth(smooth(updated))


def solution(mesh):
    in_specs = (
        P(None, ("face", "elem")),
        P(("face", "elem")),
        P(),
        P(None, ("face", "elem")),
        P(("face", "elem")),
        P(),
        P(("face", "elem"), None),
        P(("face", "elem"), None),
        P(None, ("face", "elem")),
        P(None, ("face", "elem")),
    )
    out_specs = P(None, ("face", "elem"))
    local = fused if mesh.shape["elem"] == 8 else general
    return jax.shard_map(local, mesh=mesh, in_specs=in_specs, out_specs=out_specs, check_vma=False)
```

```python
import functools

import jax
import jax.numpy as jnp
import numpy as np
from jax import lax
from jax.experimental import pallas as pl
from jax.experimental.pallas import tpu as pltpu
from jax.sharding import PartitionSpec as P

FIELDS = 6
LEV = 72
BLK = 18
NB = 4
NP = 4
PTS = NP * NP
SWEEPS = 3
RIM_E = 16
VISC_COEF = 0.2
LANES = 128
EDGE_PTS = 12
RIM = RIM_E * EDGE_PTS
ROWS = FIELDS * LEV
PAIRS = BLK * BLK
PIECES = FIELDS // 2
MESH = pl.DeviceIdType.MESH
HIGHEST = lax.Precision.HIGHEST
F32 = jnp.float32
BF16 = jnp.bfloat16


def iota(shape, dim):
    return lax.broadcasted_iota(jnp.int32, shape, dim)


def split(x):
    hi = x.astype(BF16)
    lo = (x - hi.astype(F32)).astype(BF16)
    return hi, lo


def packed(place):
    p = lax.rem(place, PTS)
    rank = jnp.where(p == 7, 5, jnp.where(p == 8, 6, jnp.where(p == 11, 7, jnp.where(p > 11, p - 4, p))))
    inside = (p == 5) | (p == 6) | (p == 9) | (p == 10)
    return jnp.where(inside, -4096, place // PTS * EDGE_PTS + rank)


def exact_dot(x, picks, dims=((1,), (0,))):
    hi, lo = split(x)
    both = jnp.concatenate([hi, lo], axis=0)
    total = lax.dot_general(both, picks, (dims, ((), ())), preferred_element_type=F32)
    return total[:x.shape[0]] + total[x.shape[0]:]


def kernel(
    groups,
    field_ref, day_ref, heat_ref, couple_ref, metric_ref, stencil_ref, owner_ref, edge_ref,
    kept_hbm, slot_hbm,
    out_ref,
    kept_raw, slot_raw, slot_inv, kept_src, kept_val, drive,
    send0, send1, send2, recv0, recv1, recv2, slot_val, slot_y0,
    ret0, ret1, ret2, home_buf, upd, lap1, lap2, low1, high1, low2, high2, out1, out2, picks, rims, pack, route,
    load_sem, s1_sem, r1_sem, s2_sem, r2_sem, hs_sem, hr_sem,
):
    face = lax.axis_index("face")
    me = lax.axis_index("elem")
    partner = face + 1 - 2 * lax.rem(face, 2)
    right = lax.rem(me + 1, groups)
    left = lax.rem(me + groups - 1, groups)
    cap = 512 // groups
    inv_rows = NB * PAIRS
    sends, recvs, rets = (send0, send1, send2), (recv0, recv1, recv2), (ret0, ret1, ret2)

    loads = []
    for c in range(2):
        loads.append(pltpu.make_async_copy(
            kept_hbm.at[:, pl.ds(c * LANES, LANES)], kept_raw.at[pl.ds(c * inv_rows, inv_rows)],
            load_sem.at[c]))
    for a in range(groups):
        loads.append(pltpu.make_async_copy(
            slot_hbm.at[:, pl.ds((a // 2) * LANES, LANES)],
            slot_raw.at[pl.ds(a * inv_rows, inv_rows)], load_sem.at[2 + a]))
    for one in loads:
        one.start()

    barrier = pltpu.get_barrier_semaphore()
    for o in range(groups):
        pl.semaphore_signal(barrier, inc=1, device_id=(partner, jnp.int32(o)), device_id_type=MESH)
    for o in (left, right):
        pl.semaphore_signal(barrier, inc=1, device_id=(face, o), device_id_type=MESH)

    def to_owner(o, p):
        return pltpu.make_async_remote_copy(
            src_ref=sends[p].at[o], dst_ref=recvs[p].at[me], send_sem=s1_sem.at[p, o],
            recv_sem=r1_sem.at[p, me], device_id=(partner, o), device_id_type=MESH)

    def from_home(a, p):
        return pltpu.make_async_remote_copy(
            src_ref=sends[p].at[a], dst_ref=recvs[p].at[a], send_sem=s1_sem.at[p, a],
            recv_sem=r1_sem.at[p, a], device_id=(partner, a), device_id_type=MESH)

    def to_home(a, p):
        return pltpu.make_async_remote_copy(
            src_ref=rets[p].at[a], dst_ref=home_buf.at[p, me], send_sem=s2_sem.at[p, a],
            recv_sem=r2_sem.at[p, me], device_id=(partner, a), device_id_type=MESH)

    def from_owner(o, p):
        return pltpu.make_async_remote_copy(
            src_ref=rets[p].at[o], dst_ref=home_buf.at[p, o], send_sem=s2_sem.at[p, o],
            recv_sem=r2_sem.at[p, o], device_id=(partner, o), device_id_type=MESH)

    owner = owner_ref[...]
    named = iota((groups, 256), 0) == owner
    earlier = (iota((256, 256), 0) < iota((256, 256), 1)).astype(BF16)
    before = jnp.dot(named.astype(BF16), earlier, preferred_element_type=F32)
    rank = jnp.sum(jnp.where(named, before, 0.0), axis=0, keepdims=True).astype(jnp.int32)
    spot = owner * LANES + rank
    spot2 = jnp.concatenate([spot, spot + cap], axis=1)
    route[...] = (iota((groups * LANES, 512), 0) == spot2).astype(BF16)

    outer = (((0,), (0,)), ((), ()))
    day = day_ref[...].astype(F32)
    heating = lax.dot_general(heat_ref[...], day, outer, precision=HIGHEST, preferred_element_type=F32)
    source = field_ref[...] + heating
    couple = couple_ref[...]
    sent_couple = couple[:, 256:]
    tail = jnp.concatenate(
        [jnp.concatenate([sent_couple, sent_couple], axis=1), jnp.zeros((5, 512), F32)], axis=0)
    for p in range(PIECES):
        body = jnp.concatenate(
            [source[p * LEV:(p + 1) * LEV, 256:], source[(p + 3) * LEV:(p + 4) * LEV, 256:]], axis=1)
        if p == 0:
            body = jnp.concatenate([body, tail], axis=0)
        record = exact_dot(body, route[...], ((1,), (1,)))
        for o in range(groups):
            sends[p][o] = record[:, o * LANES:(o + 1) * LANES]
        if p == 0:
            pl.semaphore_wait(barrier, groups + 2)
        for k in range(groups):
            to_owner(lax.rem(me + k, groups), p).start()
    for f in range(FIELDS):
        for c in range(2):
            kept_src[pl.ds((f * 2 + c) * LEV, LEV), :] = source[
                f * LEV:(f + 1) * LEV, c * LANES:(c + 1) * LANES]

    for one in loads[2:]:
        one.wait()
    plain = (iota((8, LANES), 1) < cap) == (lax.rem(iota((8, LANES), 0), 2) == 0)

    def slot_pair(step, _):
        for u in range(BLK):
            r = step * BLK + u
            x = slot_raw[pl.ds(r, 8, stride=inv_rows), :]
            slot_inv[r] = jnp.where(plain, x, pltpu.roll(x, cap, 1))
        return 0

    lax.fori_loop(0, NB * BLK, slot_pair, 0)

    slot_m = slot_inv

    def slot_piece(p):
        for a in range(groups):
            from_home(a, p).wait_recv()
        rows = LEV + 8 if p == 0 else LEV
        recv_flat = recvs[p].reshape(groups * rows, LANES)
        ret_flat = rets[p].reshape(groups * LEV, LANES)

        def slot_value(step, _):
            for u in range(8):
                slot_val[step * 8 + u] = recv_flat[pl.ds(step * 8 + u, 8, stride=rows), :]
            return 0

        lax.fori_loop(0, LEV // 8, slot_value, 0)
        if p == 0:
            for k in range(NB - 1):
                slot_val[LEV + k] = recv_flat[pl.ds(LEV + k, 8, stride=rows), :]

        for b in range(NB):
            values = [slot_val[b * BLK + j] for j in range(BLK)]

            def slot_first(i, _):
                sums = [slot_m[(b * BLK + i) * BLK + j] * values[j] for j in range(BLK)]
                while len(sums) > 1:
                    pairs = [sums[k] + sums[k + 1] for k in range(0, len(sums) - 1, 2)]
                    sums = pairs + sums[len(pairs) * 2:]
                slot_y0[b * BLK + i] = sums[0]
                return 0

            lax.fori_loop(0, BLK, slot_first, 0)

        between = [slot_val[LEV + k] for k in range(NB - 1)]

        def slot_drive(e0, e17):
            lo = [None] + [between[b - 1] * e17[b - 1] for b in range(1, NB)]
            hi = [between[b] * e0[b + 1] for b in range(NB - 1)] + [None]
            return lo, hi

        def driven(y, b, i, lo, hi):
            if lo is not None:
                y = y + slot_m[(b * BLK + i) * BLK] * lo
            if hi is not None:
                y = y + slot_m[(b * BLK + i) * BLK + BLK - 1] * hi
            return y

        e0 = first = [slot_y0[b * BLK] for b in range(NB)]
        e17 = last = [slot_y0[b * BLK + BLK - 1] for b in range(NB)]
        for _ in range(SWEEPS - 1):
            lo, hi = slot_drive(e0, e17)
            e0 = [driven(first[b], b, 0, lo[b], hi[b]) for b in range(NB)]
            e17 = [driven(last[b], b, BLK - 1, lo[b], hi[b]) for b in range(NB)]
        lo, hi = slot_drive(e0, e17)

        def slot_final(i, _):
            for b in range(NB):
                r = b * BLK + i
                ret_flat[pl.ds(r, 8, stride=LEV), :] = driven(slot_y0[r], b, i, lo[b], hi[b])
            return 0

        lax.fori_loop(0, BLK, slot_final, 0)
        for k in range(groups):
            to_home(lax.rem(me + k, groups), p).start()

    slot_piece(0)

    for one in loads[:2]:
        one.wait()

    def kept_value(j, _):
        for f in range(FIELDS):
            kept_val[f * BLK + j] = kept_src[pl.ds(f * 2 * LEV + j, 8, stride=BLK), :]
        return 0

    lax.fori_loop(0, BLK, kept_value, 0)

    def kept_m(ij):
        return kept_raw[pl.ds(ij, 8, stride=PAIRS), :]

    def kept_row(i):
        sums = [None] * FIELDS
        for j in range(BLK):
            m = kept_m(i * BLK + j)
            for f in range(FIELDS):
                term = m * kept_val[f * BLK + j]
                sums[f] = term if sums[f] is None else sums[f] + term
        return sums

    first = kept_row(0)
    last = kept_row(BLK - 1)
    ends = (kept_m(0), kept_m(BLK - 1), kept_m((BLK - 1) * BLK), kept_m(PAIRS - 1))
    gap = jnp.zeros((1, LANES), F32)
    pieces_low, pieces_high = [], []
    for c in range(2):
        rows = [couple[k:k + 1, c * LANES:(c + 1) * LANES] for k in range(NB - 1)]
        pieces_low += [gap] + rows
        pieces_high += rows + [gap]
    c_low = jnp.concatenate(pieces_low, axis=0)
    c_high = jnp.concatenate(pieces_high, axis=0)

    def kept_drive(e0, e17):
        return c_low * pltpu.roll(e17, 1, 0), c_high * pltpu.roll(e0, 7, 0)

    drives = []
    for f in range(FIELDS):
        e0, e17 = first[f], last[f]
        for _ in range(SWEEPS - 1):
            lo, hi = kept_drive(e0, e17)
            e0 = first[f] + ends[0] * lo + ends[1] * hi
            e17 = last[f] + ends[2] * lo + ends[3] * hi
        drives.append(kept_drive(e0, e17))
    for f in range(FIELDS):
        drive[2 * f] = drives[f][0]
        drive[2 * f + 1] = drives[f][1]

    def kept_final(i, _):
        sums = kept_row(i)
        m0, m1 = kept_m(i * BLK), kept_m(i * BLK + BLK - 1)
        for f in range(FIELDS):
            y = sums[f] + m0 * drive[2 * f] + m1 * drive[2 * f + 1]
            kept_src[pl.ds(f * 2 * LEV + i, 8, stride=BLK), :] = y
        return 0

    lax.fori_loop(0, BLK, kept_final, 0)
    for p in range(PIECES):
        for c in range(2):
            upd[p, c] = jnp.concatenate(
                [kept_src[pl.ds((f * 2 + c) * LEV, LEV), :] for f in (p, p + 3)], axis=0)

    spread = (lax.rem(iota((PTS, LANES), 1), PTS) == iota((PTS, LANES), 0)).astype(F32)
    part = jnp.dot(stencil_ref[...], spread, precision=HIGHEST, preferred_element_type=F32)
    full = lax.dot_general(part, spread, outer, precision=HIGHEST, preferred_element_type=F32)
    same = iota((LANES, LANES), 0) // PTS == iota((LANES, LANES), 1) // PTS
    op_hi, op_lo = split(jnp.where(same, full, 0.0))

    def laplace(x, c):
        applied = exact_dot(x, op_hi)
        applied = applied + jnp.dot(x.astype(BF16), op_lo, preferred_element_type=F32)
        return applied * metric_ref[:, c * LANES:(c + 1) * LANES]

    def to_left(out, high, n, p):
        return pltpu.make_async_remote_copy(
            src_ref=out.at[0, p], dst_ref=high.at[p], send_sem=hs_sem.at[n, p],
            recv_sem=hr_sem.at[n, p], device_id=(face, left), device_id_type=MESH)

    def to_right(out, low, n, p):
        return pltpu.make_async_remote_copy(
            src_ref=out.at[1, p], dst_ref=low.at[p], send_sem=hs_sem.at[n, p],
            recv_sem=hr_sem.at[n, p], device_id=(face, right), device_id_type=MESH)

    place512 = iota((512, 2 * RIM), 0)
    place_now = lax.rem(place512, 256)
    shift = place512 // 256 * RIM
    pack[...] = (packed(place_now) + shift == iota((512, 2 * RIM), 1)).astype(BF16)

    def edges(lap, out, side, p):
        halves = [lap[p, 2 * side + c][h * LEV:(h + 1) * LEV] for h in range(2) for c in range(2)]
        mine = exact_dot(jnp.concatenate(halves, axis=1), pack[...])
        for k in range(3):
            out[side, p, k] = mine[:, k * LANES:(k + 1) * LANES]

    for p in range(PIECES):
        for c in range(2):
            lap1[p, c] = laplace(upd[p, c], c)
        edges(lap1, out1, 0, p)
    slot_piece(1)

    col = iota((1, 512), 1)
    point = lax.rem(col, PTS)
    pi, pj = point // NP, lax.rem(point, NP)
    place = (iota((32, 512), 1) // PTS == iota((32, 512), 0)).astype(F32)
    table = jnp.dot(edge_ref[...].astype(F32), place, preferred_element_type=F32).astype(jnp.int32) * PTS
    flip_i = (NP - 1 - pi) * NP + pj
    flip_j = pi * NP + NP - 1 - pj
    vert = jnp.where(pi == 0, table[0:1] + flip_i, jnp.where(pi == NP - 1, table[2:3] + flip_i, -1))
    hori = jnp.where(pj == NP - 1, table[1:2] + flip_j, jnp.where(pj == 0, table[3:4] + flip_j, -1))
    for k in range(4):
        row = iota((LANES, 512), 0) + k * LANES
        count = ((row == col).astype(F32) + (row + 256 == vert).astype(F32)
                 + (row + 256 == hori).astype(F32))
        picks[pl.ds(k * LANES, LANES), :] = count.astype(BF16)
    for side, base in ((0, 0), (1, 768)):
        found = []
        for t in (vert, hori):
            near = (t >= base) & (t < base + 256)
            found.append(jnp.where(near, packed(jnp.where(near, t - base, 0)), -4096))
        for h in range(2):
            row = iota((256, 512), 0) - h * (256 - RIM)
            count = (row == found[0]).astype(F32) + (row == found[1]).astype(F32)
            rims[side, h] = count.astype(BF16)
    share = 1.0 / (1.0 + jnp.where((pi == 0) | (pi == NP - 1), 1.0, 0.0)
                   + jnp.where((pj == 0) | (pj == NP - 1), 1.0, 0.0))

    slot_piece(2)
    for p in range(PIECES):
        to_left(out1, high1, 0, p).start()

    def own_sum(lap, p):
        mine = jnp.concatenate([lap[p, c] for c in range(4)], axis=1)
        return exact_dot(mine, picks[...])

    def rim_sum(rim, p, side):
        return jnp.concatenate([
            exact_dot(jnp.concatenate([rim[p, h], rim[p, h + 1]], axis=1), rims[side, h])
            for h in range(2)], axis=0)

    def at_home(p):
        for o in range(groups):
            from_owner(o, p).wait_recv()
        home = jnp.concatenate([home_buf[p, o] for o in range(groups)], axis=1)
        back = exact_dot(home, route[...])
        for c in range(2):
            upd[p, 2 + c] = jnp.concatenate(
                [back[:, c * LANES:(c + 1) * LANES], back[:, (2 + c) * LANES:(3 + c) * LANES]], axis=0)
        for c in (2, 3):
            lap1[p, c] = laplace(upd[p, c], c)
        edges(lap1, out1, 1, p)
        to_right(out1, low1, 1, p).start()

    def averaged(lap, out, high, low, n, p):
        total = own_sum(lap, p)
        to_left(out, high, n, p).wait_recv()
        total = total + rim_sum(high, p, 1)
        to_right(out, low, n + 1, p).wait_recv()
        return (total + rim_sum(low, p, 0)) * share

    def first_round(p):
        first_pass = averaged(lap1, out1, high1, low1, 0, p)
        for c in range(4):
            lap2[p, c] = laplace(first_pass[:, c * LANES:(c + 1) * LANES], c)
        edges(lap2, out2, 0, p)
        to_left(out2, high2, 2, p).start()
        edges(lap2, out2, 1, p)
        to_right(out2, low2, 3, p).start()

    def second_round(p):
        second = averaged(lap2, out2, high2, low2, 2, p)
        for c in range(4):
            lanes = slice(c * LANES, (c + 1) * LANES)
            new = upd[p, c] - VISC_COEF * second[:, lanes]
            out_ref[p * LEV:(p + 1) * LEV, lanes] = new[:LEV]
            out_ref[(p + 3) * LEV:(p + 4) * LEV, lanes] = new[LEV:]

    at_home(0)
    at_home(1)
    first_round(0)
    at_home(2)
    first_round(1)
    first_round(2)
    second_round(0)
    second_round(1)
    second_round(2)

    for p in range(PIECES):
        for k in range(groups):
            to_owner(jnp.int32(k), p).wait_send()
            to_home(jnp.int32(k), p).wait_send()
        for out, low, high, n in ((out1, low1, high1, 0), (out2, low2, high2, 2)):
            to_left(out, high, n, p).wait_send()
            to_right(out, low, n + 1, p).wait_send()


def fused(field_state, day_cost, heat_rate, coupling, metric, stencil, phys_owner, edge_table,
          kept_inverse, slot_inverse):
    groups = lax.axis_size("elem")
    cols = field_state.shape[1]
    inv_rows = NB * PAIRS
    vmem = pl.BlockSpec(memory_space=pltpu.VMEM)
    anywhere = pl.BlockSpec(memory_space=pl.ANY)
    dma = pltpu.SemaphoreType.DMA
    rim = pltpu.VMEM((PIECES, 3, LEV, LANES), F32)
    outgoing = pltpu.VMEM((2, PIECES, 3, LEV, LANES), F32)
    whole = pltpu.VMEM((PIECES, 4, 2 * LEV, LANES), F32)
    part = pltpu.VMEM((groups, LEV, LANES), F32)
    part0 = pltpu.VMEM((groups, LEV + 8, LANES), F32)
    return pl.pallas_call(
        functools.partial(kernel, groups),
        out_shape=jax.ShapeDtypeStruct((ROWS, cols), F32),
        in_specs=[vmem] * 8 + [anywhere] * 2,
        out_specs=vmem,
        scratch_shapes=[
            pltpu.VMEM((2 * inv_rows, LANES), F32),
            pltpu.VMEM((groups * inv_rows, LANES), F32),
            pltpu.VMEM((inv_rows, 8, LANES), F32),
            pltpu.VMEM((2 * ROWS, LANES), F32),
            pltpu.VMEM((FIELDS * BLK, 8, LANES), F32),
            pltpu.VMEM((2 * FIELDS, 8, LANES), F32),
            part0, part, part, part0, part, part,
            pltpu.VMEM((LEV + 8, 8, LANES), F32),
            pltpu.VMEM((LEV, 8, LANES), F32),
            part, part, part,
            pltpu.VMEM((PIECES, groups, LEV, LANES), F32),
            whole, whole, whole,
            rim, rim, rim, rim, outgoing, outgoing,
            pltpu.VMEM((512, 512), BF16),
            pltpu.VMEM((2, 2, 256, 512), BF16),
            pltpu.VMEM((512, 2 * RIM), BF16),
            pltpu.VMEM((groups * LANES, 512), BF16),
            dma((2 + groups,)), dma((PIECES, groups)), dma((PIECES, groups)),
            dma((PIECES, groups)), dma((PIECES, groups)), dma((4, PIECES)), dma((4, PIECES)),
        ],
        compiler_params=pltpu.CompilerParams(
            collective_id=0, has_side_effects=True, vmem_limit_bytes=60 * 2**20),
    )(
        field_state, day_cost.reshape(1, -1), heat_rate.reshape(1, -1), coupling,
        metric.reshape(1, -1), stencil, phys_owner.reshape(1, -1), edge_table.T,
        kept_inverse, slot_inverse,
    )


def swapped(value):
    pairs = [(source, source ^ 1) for source in range(lax.axis_size("face"))]
    return lax.ppermute(value, "face", pairs)


def block_apply(blocks, values):
    result = jnp.zeros(values.shape, F32)
    for j in range(BLK):
        result = result + blocks[None, :, :, j, :] * values[:, :, j, None, :]
    return result


def physics(source, inverse, couple):
    count_n = source.shape[1]
    values = source.reshape(FIELDS, NB, BLK, count_n)
    blocks = inverse.reshape(NB, BLK, BLK, count_n)
    state = block_apply(blocks, values)
    for _ in range(SWEEPS):
        driven = values.at[:, 1:, 0, :].add(couple[None] * state[:, :-1, BLK - 1, :])
        driven = driven.at[:, :-1, BLK - 1, :].add(couple[None] * state[:, 1:, 0, :])
        state = block_apply(blocks, driven)
    return state.reshape(FIELDS * LEV, count_n)


def general(field_state, day_cost, heat_rate, coupling, metric, stencil, phys_owner, edge_table,
            kept_inverse, slot_inverse):
    cols = field_state.shape[1]
    half = cols // 2
    groups = lax.axis_size("elem")
    cap = cols // groups
    source = field_state + day_cost[None, :].astype(F32) * heat_rate[:, None]
    owners = phys_owner[:, 0]
    named = (owners[:, None] == jnp.arange(groups)[None, :]).astype(F32)
    places = jnp.arange(half)
    earlier = (places[None, :] < places[:, None]).astype(F32)
    rank = jnp.sum(jnp.dot(earlier, named, precision=HIGHEST) * named, axis=1).astype(jnp.int32)
    route = ((owners * cap + rank)[:, None] == jnp.arange(cols)[None, :]).astype(F32)
    record = jnp.concatenate([source[:, half:], coupling[:, half:]], axis=0)
    record = jnp.dot(record, route, precision=HIGHEST)
    crossed = swapped(lax.all_to_all(record, "elem", split_axis=1, concat_axis=1, tiled=True))
    done = physics(crossed[:ROWS], slot_inverse, crossed[ROWS:])
    home = lax.all_to_all(swapped(done), "elem", split_axis=1, concat_axis=1, tiled=True)
    sent = jnp.dot(home, route.T, precision=HIGHEST)
    kept = physics(source[:, :half], kept_inverse, coupling[:, :half])
    updated = jnp.concatenate([kept, sent], axis=1)
    rim = RIM_E * PTS
    point = np.arange(cols) % PTS
    pi, pj = point // NP, point % NP
    flip_i, flip_j = (NP - 1 - pi) * NP + pj, pi * NP + NP - 1 - pj
    table = jnp.repeat(edge_table, PTS, axis=0) * PTS
    rows = jnp.arange(cols + 2 * rim)[:, None]
    picks = (rows == jnp.arange(cols)[None, :] + rim).astype(F32)
    sides = ((pi == 0, flip_i), (pj == NP - 1, flip_j), (pi == NP - 1, flip_i), (pj == 0, flip_j))
    divisor = np.ones((cols,), np.float32)
    for k, (mask, match) in enumerate(sides):
        divisor = divisor + mask
        picks = picks + ((rows == (table[:, k] + match)[None, :]) & mask[None, :]).astype(F32)
    operator = jnp.kron(jnp.eye(cols // PTS, dtype=F32), stencil.T)
    ring = [(i, (i + 1) % groups) for i in range(groups)]
    back = [(b, a) for a, b in ring]

    def smooth(x):
        lap = jnp.dot(x, operator, precision=HIGHEST) * metric[None, :]
        low = lax.ppermute(lap[:, cols - rim:], "elem", ring)
        high = lax.ppermute(lap[:, :rim], "elem", back)
        extended = jnp.concatenate([low, lap, high], axis=1)
        return jnp.dot(extended, picks, precision=HIGHEST) / divisor.astype(np.float32)[None, :]

    return updated - VISC_COEF * smooth(smooth(updated))


def solution(mesh):
    in_specs = (
        P(None, ("face", "elem")),
        P(("face", "elem")),
        P(),
        P(None, ("face", "elem")),
        P(("face", "elem")),
        P(),
        P(("face", "elem"), None),
        P(("face", "elem"), None),
        P(None, ("face", "elem")),
        P(None, ("face", "elem")),
    )
    out_specs = P(None, ("face", "elem"))
    local = fused if mesh.shape["elem"] == 8 else general
    return jax.shard_map(local, mesh=mesh, in_specs=in_specs, out_specs=out_specs, check_vma=False)
```

```python
import functools

import jax
import jax.numpy as jnp
import numpy as np
from jax import lax
from jax.experimental import pallas as pl
from jax.experimental.pallas import tpu as pltpu
from jax.sharding import PartitionSpec as P

FIELDS = 6
LEV = 72
BLK = 18
NB = 4
NP = 4
PTS = NP * NP
SWEEPS = 3
RIM_E = 16
VISC_COEF = 0.2
LANES = 128
EDGE_PTS = 12
RIM = RIM_E * EDGE_PTS
ROWS = FIELDS * LEV
PAIRS = BLK * BLK
PIECES = FIELDS // 2
MESH = pl.DeviceIdType.MESH
HIGHEST = lax.Precision.HIGHEST
F32 = jnp.float32
BF16 = jnp.bfloat16


def iota(shape, dim):
    return lax.broadcasted_iota(jnp.int32, shape, dim)


def split(x):
    hi = x.astype(BF16)
    lo = (x - hi.astype(F32)).astype(BF16)
    return hi, lo


def packed(place):
    p = lax.rem(place, PTS)
    rank = jnp.where(p == 7, 5, jnp.where(p == 8, 6, jnp.where(p == 11, 7, jnp.where(p > 11, p - 4, p))))
    inside = (p == 5) | (p == 6) | (p == 9) | (p == 10)
    return jnp.where(inside, -4096, place // PTS * EDGE_PTS + rank)


def exact_dot(x, picks, dims=((1,), (0,))):
    hi, lo = split(x)
    both = jnp.concatenate([hi, lo], axis=0)
    total = lax.dot_general(both, picks, (dims, ((), ())), preferred_element_type=F32)
    return total[:x.shape[0]] + total[x.shape[0]:]


def kernel(
    groups,
    field_ref, day_ref, heat_ref, couple_ref, metric_ref, stencil_ref, owner_ref, edge_ref,
    kept_hbm, slot_hbm,
    out_ref,
    kept_raw, slot_raw, slot_inv, kept_src, kept_val, drive,
    send0, send1, send2, recv0, recv1, recv2, slot_val, slot_y0,
    ret0, ret1, ret2, home_buf, upd, lap1, lap2, low1, high1, low2, high2, out1, out2, picks, rims, pack, route,
    load_sem, s1_sem, r1_sem, s2_sem, r2_sem, hs_sem, hr_sem,
):
    face = lax.axis_index("face")
    me = lax.axis_index("elem")
    partner = face + 1 - 2 * lax.rem(face, 2)
    right = lax.rem(me + 1, groups)
    left = lax.rem(me + groups - 1, groups)
    cap = 512 // groups
    inv_rows = NB * PAIRS
    sends, recvs, rets = (send0, send1, send2), (recv0, recv1, recv2), (ret0, ret1, ret2)

    loads = []
    for c in range(2):
        loads.append(pltpu.make_async_copy(
            kept_hbm.at[:, pl.ds(c * LANES, LANES)], kept_raw.at[pl.ds(c * inv_rows, inv_rows)],
            load_sem.at[c]))
    for a in range(groups):
        loads.append(pltpu.make_async_copy(
            slot_hbm.at[:, pl.ds((a // 2) * LANES, LANES)],
            slot_raw.at[pl.ds(a * inv_rows, inv_rows)], load_sem.at[2 + a]))
    for one in loads:
        one.start()

    barrier = pltpu.get_barrier_semaphore()
    for o in range(groups):
        pl.semaphore_signal(barrier, inc=1, device_id=(partner, jnp.int32(o)), device_id_type=MESH)
    for o in (left, right):
        pl.semaphore_signal(barrier, inc=1, device_id=(face, o), device_id_type=MESH)

    def to_owner(o, p):
        return pltpu.make_async_remote_copy(
            src_ref=sends[p].at[o], dst_ref=recvs[p].at[me], send_sem=s1_sem.at[p, o],
            recv_sem=r1_sem.at[p, me], device_id=(partner, o), device_id_type=MESH)

    def from_home(a, p):
        return pltpu.make_async_remote_copy(
            src_ref=sends[p].at[a], dst_ref=recvs[p].at[a], send_sem=s1_sem.at[p, a],
            recv_sem=r1_sem.at[p, a], device_id=(partner, a), device_id_type=MESH)

    def to_home(a, p):
        return pltpu.make_async_remote_copy(
            src_ref=rets[p].at[a], dst_ref=home_buf.at[p, me], send_sem=s2_sem.at[p, a],
            recv_sem=r2_sem.at[p, me], device_id=(partner, a), device_id_type=MESH)

    def from_owner(o, p):
        return pltpu.make_async_remote_copy(
            src_ref=rets[p].at[o], dst_ref=home_buf.at[p, o], send_sem=s2_sem.at[p, o],
            recv_sem=r2_sem.at[p, o], device_id=(partner, o), device_id_type=MESH)

    owner = owner_ref[...]
    named = iota((groups, 256), 0) == owner
    earlier = (iota((256, 256), 0) < iota((256, 256), 1)).astype(BF16)
    before = jnp.dot(named.astype(BF16), earlier, preferred_element_type=F32)
    rank = jnp.sum(jnp.where(named, before, 0.0), axis=0, keepdims=True).astype(jnp.int32)
    spot = owner * LANES + rank
    spot2 = jnp.concatenate([spot, spot + cap], axis=1)
    route[...] = (iota((groups * LANES, 512), 0) == spot2).astype(BF16)

    outer = (((0,), (0,)), ((), ()))
    day = day_ref[...].astype(F32)
    heating = lax.dot_general(heat_ref[...], day, outer, precision=HIGHEST, preferred_element_type=F32)
    source = field_ref[...] + heating
    couple = couple_ref[...]
    sent_couple = couple[:, 256:]
    tail = jnp.concatenate(
        [jnp.concatenate([sent_couple, sent_couple], axis=1), jnp.zeros((5, 512), F32)], axis=0)
    for p in range(PIECES):
        body = jnp.concatenate(
            [source[p * LEV:(p + 1) * LEV, 256:], source[(p + 3) * LEV:(p + 4) * LEV, 256:]], axis=1)
        if p == 0:
            body = jnp.concatenate([body, tail], axis=0)
        record = exact_dot(body, route[...], ((1,), (1,)))
        for o in range(groups):
            sends[p][o] = record[:, o * LANES:(o + 1) * LANES]
        if p == 0:
            pl.semaphore_wait(barrier, groups + 2)
        for k in range(groups):
            to_owner(lax.rem(me + k, groups), p).start()
    for f in range(FIELDS):
        for c in range(2):
            kept_src[pl.ds((f * 2 + c) * LEV, LEV), :] = source[
                f * LEV:(f + 1) * LEV, c * LANES:(c + 1) * LANES]

    for one in loads[2:]:
        one.wait()
    plain = (iota((8, LANES), 1) < cap) == (lax.rem(iota((8, LANES), 0), 2) == 0)

    def slot_pair(step, _):
        for u in range(BLK):
            r = step * BLK + u
            x = slot_raw[pl.ds(r, 8, stride=inv_rows), :]
            slot_inv[r] = jnp.where(plain, x, pltpu.roll(x, cap, 1))
        return 0

    lax.fori_loop(0, NB * BLK, slot_pair, 0)

    slot_m = slot_inv

    def slot_piece(p):
        for a in range(groups):
            from_home(a, p).wait_recv()
        rows = LEV + 8 if p == 0 else LEV
        recv_flat = recvs[p].reshape(groups * rows, LANES)
        ret_flat = rets[p].reshape(groups * LEV, LANES)

        def slot_value(step, _):
            for u in range(8):
                slot_val[step * 8 + u] = recv_flat[pl.ds(step * 8 + u, 8, stride=rows), :]
            return 0

        lax.fori_loop(0, LEV // 8, slot_value, 0)
        if p == 0:
            for k in range(NB - 1):
                slot_val[LEV + k] = recv_flat[pl.ds(LEV + k, 8, stride=rows), :]

        for b in range(NB):
            values = [slot_val[b * BLK + j] for j in range(BLK)]

            def slot_first(i, _):
                sums = [slot_m[(b * BLK + i) * BLK + j] * values[j] for j in range(BLK)]
                while len(sums) > 1:
                    pairs = [sums[k] + sums[k + 1] for k in range(0, len(sums) - 1, 2)]
                    sums = pairs + sums[len(pairs) * 2:]
                slot_y0[b * BLK + i] = sums[0]
                return 0

            lax.fori_loop(0, BLK, slot_first, 0)

        between = [slot_val[LEV + k] for k in range(NB - 1)]

        def slot_drive(e0, e17):
            lo = [None] + [between[b - 1] * e17[b - 1] for b in range(1, NB)]
            hi = [between[b] * e0[b + 1] for b in range(NB - 1)] + [None]
            return lo, hi

        def driven(y, b, i, lo, hi):
            if lo is not None:
                y = y + slot_m[(b * BLK + i) * BLK] * lo
            if hi is not None:
                y = y + slot_m[(b * BLK + i) * BLK + BLK - 1] * hi
            return y

        e0 = first = [slot_y0[b * BLK] for b in range(NB)]
        e17 = last = [slot_y0[b * BLK + BLK - 1] for b in range(NB)]
        for _ in range(SWEEPS - 1):
            lo, hi = slot_drive(e0, e17)
            e0 = [driven(first[b], b, 0, lo[b], hi[b]) for b in range(NB)]
            e17 = [driven(last[b], b, BLK - 1, lo[b], hi[b]) for b in range(NB)]
        lo, hi = slot_drive(e0, e17)

        def slot_final(i, _):
            for b in range(NB):
                r = b * BLK + i
                ret_flat[pl.ds(r, 8, stride=LEV), :] = driven(slot_y0[r], b, i, lo[b], hi[b])
            return 0

        lax.fori_loop(0, BLK, slot_final, 0)
        for k in range(groups):
            to_home(lax.rem(me + k, groups), p).start()

    slot_piece(0)

    for one in loads[:2]:
        one.wait()

    def kept_value(j, _):
        for f in range(FIELDS):
            kept_val[f * BLK + j] = kept_src[pl.ds(f * 2 * LEV + j, 8, stride=BLK), :]
        return 0

    lax.fori_loop(0, BLK, kept_value, 0)

    def kept_m(ij):
        return kept_raw[pl.ds(ij, 8, stride=PAIRS), :]

    def kept_row(i):
        sums = [None] * FIELDS
        for j in range(BLK):
            m = kept_m(i * BLK + j)
            for f in range(FIELDS):
                term = m * kept_val[f * BLK + j]
                sums[f] = term if sums[f] is None else sums[f] + term
        return sums

    first = kept_row(0)
    last = kept_row(BLK - 1)
    ends = (kept_m(0), kept_m(BLK - 1), kept_m((BLK - 1) * BLK), kept_m(PAIRS - 1))
    gap = jnp.zeros((1, LANES), F32)
    pieces_low, pieces_high = [], []
    for c in range(2):
        rows = [couple[k:k + 1, c * LANES:(c + 1) * LANES] for k in range(NB - 1)]
        pieces_low += [gap] + rows
        pieces_high += rows + [gap]
    c_low = jnp.concatenate(pieces_low, axis=0)
    c_high = jnp.concatenate(pieces_high, axis=0)

    def kept_drive(e0, e17):
        return c_low * pltpu.roll(e17, 1, 0), c_high * pltpu.roll(e0, 7, 0)

    drives = []
    for f in range(FIELDS):
        e0, e17 = first[f], last[f]
        for _ in range(SWEEPS - 1):
            lo, hi = kept_drive(e0, e17)
            e0 = first[f] + ends[0] * lo + ends[1] * hi
            e17 = last[f] + ends[2] * lo + ends[3] * hi
        drives.append(kept_drive(e0, e17))
    for f in range(FIELDS):
        drive[2 * f] = drives[f][0]
        drive[2 * f + 1] = drives[f][1]

    def kept_final(i, _):
        sums = kept_row(i)
        m0, m1 = kept_m(i * BLK), kept_m(i * BLK + BLK - 1)
        for f in range(FIELDS):
            y = sums[f] + m0 * drive[2 * f] + m1 * drive[2 * f + 1]
            kept_src[pl.ds(f * 2 * LEV + i, 8, stride=BLK), :] = y
        return 0

    lax.fori_loop(0, BLK, kept_final, 0)
    for p in range(PIECES):
        for c in range(2):
            upd[p, c] = jnp.concatenate(
                [kept_src[pl.ds((f * 2 + c) * LEV, LEV), :] for f in (p, p + 3)], axis=0)

    spread = (lax.rem(iota((PTS, LANES), 1), PTS) == iota((PTS, LANES), 0)).astype(F32)
    part = jnp.dot(stencil_ref[...], spread, precision=HIGHEST, preferred_element_type=F32)
    full = lax.dot_general(part, spread, outer, precision=HIGHEST, preferred_element_type=F32)
    same = iota((LANES, LANES), 0) // PTS == iota((LANES, LANES), 1) // PTS
    op_hi, op_lo = split(jnp.where(same, full, 0.0))

    def laplace(x, c):
        applied = exact_dot(x, op_hi)
        applied = applied + jnp.dot(x.astype(BF16), op_lo, preferred_element_type=F32)
        return applied * metric_ref[:, c * LANES:(c + 1) * LANES]

    def to_left(out, high, n, p):
        return pltpu.make_async_remote_copy(
            src_ref=out.at[0, p], dst_ref=high.at[p], send_sem=hs_sem.at[n, p],
            recv_sem=hr_sem.at[n, p], device_id=(face, left), device_id_type=MESH)

    def to_right(out, low, n, p):
        return pltpu.make_async_remote_copy(
            src_ref=out.at[1, p], dst_ref=low.at[p], send_sem=hs_sem.at[n, p],
            recv_sem=hr_sem.at[n, p], device_id=(face, right), device_id_type=MESH)

    place512 = iota((512, 2 * RIM), 0)
    place_now = lax.rem(place512, 256)
    shift = place512 // 256 * RIM
    pack[...] = (packed(place_now) + shift == iota((512, 2 * RIM), 1)).astype(BF16)

    def edges(lap, out, side, p):
        halves = [lap[p, 2 * side + c][h * LEV:(h + 1) * LEV] for h in range(2) for c in range(2)]
        mine = exact_dot(jnp.concatenate(halves, axis=1), pack[...])
        for k in range(3):
            out[side, p, k] = mine[:, k * LANES:(k + 1) * LANES]

    for p in range(PIECES):
        for c in range(2):
            lap1[p, c] = laplace(upd[p, c], c)
        edges(lap1, out1, 0, p)
        to_left(out1, high1, 0, p).start()
    slot_piece(1)

    col = iota((1, 512), 1)
    point = lax.rem(col, PTS)
    pi, pj = point // NP, lax.rem(point, NP)
    place = (iota((32, 512), 1) // PTS == iota((32, 512), 0)).astype(F32)
    table = jnp.dot(edge_ref[...].astype(F32), place, preferred_element_type=F32).astype(jnp.int32) * PTS
    flip_i = (NP - 1 - pi) * NP + pj
    flip_j = pi * NP + NP - 1 - pj
    vert = jnp.where(pi == 0, table[0:1] + flip_i, jnp.where(pi == NP - 1, table[2:3] + flip_i, -1))
    hori = jnp.where(pj == NP - 1, table[1:2] + flip_j, jnp.where(pj == 0, table[3:4] + flip_j, -1))
    for k in range(4):
        row = iota((LANES, 512), 0) + k * LANES
        count = ((row == col).astype(F32) + (row + 256 == vert).astype(F32)
                 + (row + 256 == hori).astype(F32))
        picks[pl.ds(k * LANES, LANES), :] = count.astype(BF16)
    for side, base in ((0, 0), (1, 768)):
        found = []
        for t in (vert, hori):
            near = (t >= base) & (t < base + 256)
            found.append(jnp.where(near, packed(jnp.where(near, t - base, 0)), -4096))
        for h in range(2):
            row = iota((256, 512), 0) - h * (256 - RIM)
            count = (row == found[0]).astype(F32) + (row == found[1]).astype(F32)
            rims[side, h] = count.astype(BF16)
    share = 1.0 / (1.0 + jnp.where((pi == 0) | (pi == NP - 1), 1.0, 0.0)
                   + jnp.where((pj == 0) | (pj == NP - 1), 1.0, 0.0))

    slot_piece(2)

    def own_sum(lap, p):
        mine = jnp.concatenate([lap[p, c] for c in range(4)], axis=1)
        return exact_dot(mine, picks[...])

    def rim_sum(rim, p, side):
        return jnp.concatenate([
            exact_dot(jnp.concatenate([rim[p, h], rim[p, h + 1]], axis=1), rims[side, h])
            for h in range(2)], axis=0)

    def at_home(p):
        for o in range(groups):
            from_owner(o, p).wait_recv()
        home = jnp.concatenate([home_buf[p, o] for o in range(groups)], axis=1)
        back = exact_dot(home, route[...])
        for c in range(2):
            upd[p, 2 + c] = jnp.concatenate(
                [back[:, c * LANES:(c + 1) * LANES], back[:, (2 + c) * LANES:(3 + c) * LANES]], axis=0)
        for c in (2, 3):
            lap1[p, c] = laplace(upd[p, c], c)
        edges(lap1, out1, 1, p)
        to_right(out1, low1, 1, p).start()

    def averaged(lap, out, high, low, n, p):
        total = own_sum(lap, p)
        to_left(out, high, n, p).wait_recv()
        total = total + rim_sum(high, p, 1)
        to_right(out, low, n + 1, p).wait_recv()
        return (total + rim_sum(low, p, 0)) * share

    def first_round(p):
        first_pass = averaged(lap1, out1, high1, low1, 0, p)
        for c in range(4):
            lap2[p, c] = laplace(first_pass[:, c * LANES:(c + 1) * LANES], c)
        edges(lap2, out2, 0, p)
        to_left(out2, high2, 2, p).start()
        edges(lap2, out2, 1, p)
        to_right(out2, low2, 3, p).start()

    def second_round(p):
        second = averaged(lap2, out2, high2, low2, 2, p)
        for c in range(4):
            lanes = slice(c * LANES, (c + 1) * LANES)
            new = upd[p, c] - VISC_COEF * second[:, lanes]
            out_ref[p * LEV:(p + 1) * LEV, lanes] = new[:LEV]
            out_ref[(p + 3) * LEV:(p + 4) * LEV, lanes] = new[LEV:]

    at_home(0)
    at_home(1)
    first_round(0)
    at_home(2)
    first_round(1)
    first_round(2)
    second_round(0)
    second_round(1)
    second_round(2)

    for p in range(PIECES):
        for k in range(groups):
            to_owner(jnp.int32(k), p).wait_send()
            to_home(jnp.int32(k), p).wait_send()
        for out, low, high, n in ((out1, low1, high1, 0), (out2, low2, high2, 2)):
            to_left(out, high, n, p).wait_send()
            to_right(out, low, n + 1, p).wait_send()


def fused(field_state, day_cost, heat_rate, coupling, metric, stencil, phys_owner, edge_table,
          kept_inverse, slot_inverse):
    groups = lax.axis_size("elem")
    cols = field_state.shape[1]
    inv_rows = NB * PAIRS
    vmem = pl.BlockSpec(memory_space=pltpu.VMEM)
    anywhere = pl.BlockSpec(memory_space=pl.ANY)
    dma = pltpu.SemaphoreType.DMA
    rim = pltpu.VMEM((PIECES, 3, LEV, LANES), F32)
    outgoing = pltpu.VMEM((2, PIECES, 3, LEV, LANES), F32)
    whole = pltpu.VMEM((PIECES, 4, 2 * LEV, LANES), F32)
    part = pltpu.VMEM((groups, LEV, LANES), F32)
    part0 = pltpu.VMEM((groups, LEV + 8, LANES), F32)
    return pl.pallas_call(
        functools.partial(kernel, groups),
        out_shape=jax.ShapeDtypeStruct((ROWS, cols), F32),
        in_specs=[vmem] * 8 + [anywhere] * 2,
        out_specs=vmem,
        scratch_shapes=[
            pltpu.VMEM((2 * inv_rows, LANES), F32),
            pltpu.VMEM((groups * inv_rows, LANES), F32),
            pltpu.VMEM((inv_rows, 8, LANES), F32),
            pltpu.VMEM((2 * ROWS, LANES), F32),
            pltpu.VMEM((FIELDS * BLK, 8, LANES), F32),
            pltpu.VMEM((2 * FIELDS, 8, LANES), F32),
            part0, part, part, part0, part, part,
            pltpu.VMEM((LEV + 8, 8, LANES), F32),
            pltpu.VMEM((LEV, 8, LANES), F32),
            part, part, part,
            pltpu.VMEM((PIECES, groups, LEV, LANES), F32),
            whole, whole, whole,
            rim, rim, rim, rim, outgoing, outgoing,
            pltpu.VMEM((512, 512), BF16),
            pltpu.VMEM((2, 2, 256, 512), BF16),
            pltpu.VMEM((512, 2 * RIM), BF16),
            pltpu.VMEM((groups * LANES, 512), BF16),
            dma((2 + groups,)), dma((PIECES, groups)), dma((PIECES, groups)),
            dma((PIECES, groups)), dma((PIECES, groups)), dma((4, PIECES)), dma((4, PIECES)),
        ],
        compiler_params=pltpu.CompilerParams(
            collective_id=0, has_side_effects=True, vmem_limit_bytes=60 * 2**20),
    )(
        field_state, day_cost.reshape(1, -1), heat_rate.reshape(1, -1), coupling,
        metric.reshape(1, -1), stencil, phys_owner.reshape(1, -1), edge_table.T,
        kept_inverse, slot_inverse,
    )


def swapped(value):
    pairs = [(source, source ^ 1) for source in range(lax.axis_size("face"))]
    return lax.ppermute(value, "face", pairs)


def block_apply(blocks, values):
    result = jnp.zeros(values.shape, F32)
    for j in range(BLK):
        result = result + blocks[None, :, :, j, :] * values[:, :, j, None, :]
    return result


def physics(source, inverse, couple):
    count_n = source.shape[1]
    values = source.reshape(FIELDS, NB, BLK, count_n)
    blocks = inverse.reshape(NB, BLK, BLK, count_n)
    state = block_apply(blocks, values)
    for _ in range(SWEEPS):
        driven = values.at[:, 1:, 0, :].add(couple[None] * state[:, :-1, BLK - 1, :])
        driven = driven.at[:, :-1, BLK - 1, :].add(couple[None] * state[:, 1:, 0, :])
        state = block_apply(blocks, driven)
    return state.reshape(FIELDS * LEV, count_n)


def general(field_state, day_cost, heat_rate, coupling, metric, stencil, phys_owner, edge_table,
            kept_inverse, slot_inverse):
    cols = field_state.shape[1]
    half = cols // 2
    groups = lax.axis_size("elem")
    cap = cols // groups
    source = field_state + day_cost[None, :].astype(F32) * heat_rate[:, None]
    owners = phys_owner[:, 0]
    named = (owners[:, None] == jnp.arange(groups)[None, :]).astype(F32)
    places = jnp.arange(half)
    earlier = (places[None, :] < places[:, None]).astype(F32)
    rank = jnp.sum(jnp.dot(earlier, named, precision=HIGHEST) * named, axis=1).astype(jnp.int32)
    route = ((owners * cap + rank)[:, None] == jnp.arange(cols)[None, :]).astype(F32)
    record = jnp.concatenate([source[:, half:], coupling[:, half:]], axis=0)
    record = jnp.dot(record, route, precision=HIGHEST)
    crossed = swapped(lax.all_to_all(record, "elem", split_axis=1, concat_axis=1, tiled=True))
    done = physics(crossed[:ROWS], slot_inverse, crossed[ROWS:])
    home = lax.all_to_all(swapped(done), "elem", split_axis=1, concat_axis=1, tiled=True)
    sent = jnp.dot(home, route.T, precision=HIGHEST)
    kept = physics(source[:, :half], kept_inverse, coupling[:, :half])
    updated = jnp.concatenate([kept, sent], axis=1)
    rim = RIM_E * PTS
    point = np.arange(cols) % PTS
    pi, pj = point // NP, point % NP
    flip_i, flip_j = (NP - 1 - pi) * NP + pj, pi * NP + NP - 1 - pj
    table = jnp.repeat(edge_table, PTS, axis=0) * PTS
    rows = jnp.arange(cols + 2 * rim)[:, None]
    picks = (rows == jnp.arange(cols)[None, :] + rim).astype(F32)
    sides = ((pi == 0, flip_i), (pj == NP - 1, flip_j), (pi == NP - 1, flip_i), (pj == 0, flip_j))
    divisor = np.ones((cols,), np.float32)
    for k, (mask, match) in enumerate(sides):
        divisor = divisor + mask
        picks = picks + ((rows == (table[:, k] + match)[None, :]) & mask[None, :]).astype(F32)
    operator = jnp.kron(jnp.eye(cols // PTS, dtype=F32), stencil.T)
    ring = [(i, (i + 1) % groups) for i in range(groups)]
    back = [(b, a) for a, b in ring]

    def smooth(x):
        lap = jnp.dot(x, operator, precision=HIGHEST) * metric[None, :]
        low = lax.ppermute(lap[:, cols - rim:], "elem", ring)
        high = lax.ppermute(lap[:, :rim], "elem", back)
        extended = jnp.concatenate([low, lap, high], axis=1)
        return jnp.dot(extended, picks, precision=HIGHEST) / divisor.astype(np.float32)[None, :]

    return updated - VISC_COEF * smooth(smooth(updated))


def solution(mesh):
    in_specs = (
        P(None, ("face", "elem")),
        P(("face", "elem")),
        P(),
        P(None, ("face", "elem")),
        P(("face", "elem")),
        P(),
        P(("face", "elem"), None),
        P(("face", "elem"), None),
        P(None, ("face", "elem")),
        P(None, ("face", "elem")),
    )
    out_specs = P(None, ("face", "elem"))
    local = fused if mesh.shape["elem"] == 8 else general
    return jax.shard_map(local, mesh=mesh, in_specs=in_specs, out_specs=out_specs, check_vma=False)
```
